1024 devices in a mesh: node: 64 (over z, y), local: 16 (over x, core).
Axes of the slice: x: 8, y: 8, z: 8, core: 2. Of those that a mesh axis runs over, the one named last changes fastest.
Arguments:
- grad_out: bfloat16 [8192, 7168], P('node', 'local'), may hold values from -6 to 6
- route_expert: int32 [8192, 2], P('node'), may hold values from 0 to 31, all different within a row; in each aligned block of 128 rows (0 to 127, 128 to 255, ...) at most 10 rows name the same one
- gate_prob: float32 [8192, 2], P('node'), may hold values from 0.05 to 1
- saved_gate: bfloat16 [64, 1024, 640], P('node'), may hold values from -6 to 6
- saved_up: bfloat16 [64, 1024, 640], P('node'), may hold values from -6 to 6
- w_gate: bfloat16 [64, 7168, 1024], P('node', 'local'), may hold values from -0.125 to 0.125
- w_up: bfloat16 [64, 7168, 1024], P('node', 'local'), may hold values from -0.125 to 0.125
- w_down: bfloat16 [64, 1024, 7168], P('node', None, 'local'), may hold values from -0.03125 to 0.03125
Outputs:
- grad_in: bfloat16 [8192, 7168], P('node', 'local')
- grad_prob: bfloat16 [8192, 2], P('node')
The draws below stay inside these ranges and needn't reach their ends.
Inputs may be any that keep to these rules, and one draw needn't show every extreme that they name: `route_expert`: A token names 2 different experts. Among the 128 tokens of one node group no expert is named more than 10 times, a bound that some block reaches.
All inputs are finite; a program needn't handle non-finite values.
Results may differ from the reference program's by a relative error of at most 0.027.
Values may be sent and summed in bfloat16 or wider, within the bound.
No kernel may reach another device: no remote copies, remote signals or barrier semaphores. Data moves between devices by JAX's collectives and lax.ppermute only.
A program may use at most 32 MiB of HBM per device.

```python
import math
import jax
import jax.numpy as jnp
import numpy as np
from jax import lax

D = 7168
FF = 2048
TOK_NODE = 128
TOPK = 2
EXPERTS = 32
HALF = 1024
CAP = 10
SLOTS = 640
FEAT = 448
TOKENS = 8192
N_NODE = 64
N_LOCAL = 16


def steps_of(rng, shape, cuts, least, top_value):
    level, own = 1.0, jax.random.fold_in(rng, 6)
    for position, shards_of in cuts:
        draws = jnp.exp(jax.random.uniform(jax.random.fold_in(own, position), (shards_of,), jnp.float32, least / len(cuts), top_value / len(cuts)))
        level = level * jnp.repeat(draws, shape[position] // shards_of).reshape([-1 if axis == position else 1 for axis in range(len(shape))])
    return level


def routed_block(own_key, own, number, rows, number_of, top, bound, lean):
    sequence = jax.random.permutation(own_key, number_of)
    packed, ordinary = shares(number_of, rows * top, bound, lean, True), shares(number_of, rows * top, bound, lean, False)
    places = jnp.arange(number_of)

    def named(lengths, rotation):
        used = int((lengths > 0).sum())
        fixed = max(1, used // 4)
        passed = fixed + (places - fixed + rotation * (used - fixed)) % max(1, number_of - fixed)
        return jnp.zeros((number_of,), jnp.int32).at[sequence[jnp.where(places < fixed, places, passed)]].set(jnp.asarray(lengths, jnp.int32))

    lengths = jnp.where(number % 4 == 0, named(packed, number // 4), named(ordinary, number - number // 4 - 1))
    mixed = jax.random.permutation(jax.random.fold_in(own, 3), number_of)
    giver, receiver = mixed[0:number_of // 2 * 2:2], mixed[1:number_of // 2 * 2:2]
    slack = jnp.minimum(lengths[giver] - 1, bound - lengths[receiver]) // 2
    slack = jnp.where((giver == sequence[0]) | (receiver == sequence[0]) | (lengths[receiver] == 0), 0, jnp.maximum(slack, 0))
    passed = jax.random.randint(jax.random.fold_in(own, 4), (number_of // 2,), 0, 1 << 20) % (slack + 1)
    lengths = lengths.at[giver].add(-passed).at[receiver].add(passed)
    items = jnp.searchsorted(jnp.cumsum(lengths), jnp.arange(rows * top), side="right").astype(jnp.int32)
    listing = items.reshape(top, rows).T
    listing = listing[jax.random.permutation(jax.random.fold_in(own, 1), rows)]
    rotation = jax.random.randint(jax.random.fold_in(own, 2), (rows, 1), 0, top)
    return jnp.take_along_axis(listing, (jnp.arange(top)[None, :] + rotation) % top, axis=1)


def shares(number_of, total, reach, lean, full):
    weights = [(1 << 20) // math.isqrt(standing ** lean) + 1 for standing in range(1, number_of + 1)]
    largest = reach if full else min(reach, max(-(-total // number_of), total * weights[0] // sum(weights)))
    least = 1 if total - largest >= number_of - 1 else 0
    counts, rest = [largest] + [least] * (number_of - 1), total - largest - least * (number_of - 1)
    while rest > 0:
        movable = [i for i in range(1, number_of) if counts[i] < largest] or [i for i in range(1, number_of) if counts[i] < reach]
        whole, budget = sum([weights[i] for i in movable]), rest
        for i in movable:
            more = min(reach - counts[i], max(1, budget * weights[i] // whole), rest)
            counts[i] = counts[i] + more
            rest = rest - more
    return np.array(counts)


def centred(key, dims, scale, reach, shards=(), kind=jnp.bfloat16):
    gain = steps_of(key, dims, shards, -0.22, 0.18) if shards else 1.0
    entries = jax.random.normal(key, dims, jnp.float32) * scale * gain
    return jnp.minimum(jnp.maximum(entries, -reach), reach).astype(kind)


def setup_inputs(seed: int = 0) -> dict:
    arg_keys = jax.random.split(jax.random.key(seed), 9)
    grad_out = centred(arg_keys[0], (TOKENS, D), 1.0, 6.0, ((0, 64), (1, 16)))
    route_expert_keys = jax.random.split(jax.random.fold_in(arg_keys[1], 1), TOKENS // TOK_NODE)
    route_expert_turns = jax.random.permutation(jax.random.fold_in(arg_keys[1], 3), TOKENS // TOK_NODE)
    route_expert = jax.vmap(lambda own, number: routed_block(jax.random.fold_in(arg_keys[1], 2), own, number, TOK_NODE, EXPERTS, TOPK, CAP, 2))(route_expert_keys, route_expert_turns).reshape((TOKENS, TOPK))
    gate_prob = jnp.clip(0.05 + 0.95 * jax.random.uniform(arg_keys[2], (TOKENS, TOPK), jnp.float32) ** steps_of(arg_keys[2], (TOKENS, TOPK), ((0, 64),), -0.2, 0.2), 0.05, 1.0)
    saved_gate = centred(arg_keys[3], (N_NODE, HALF, SLOTS), 1.5, 6.0, ((0, 64),))
    saved_up = centred(arg_keys[4], (N_NODE, HALF, SLOTS), 1.0, 6.0, ((0, 64),))
    w_gate = centred(arg_keys[5], (N_NODE, D, HALF), FF ** -0.5, 0.125, ((0, 64), (1, 16)))
    w_up = centred(arg_keys[6], (N_NODE, D, HALF), FF ** -0.5, 0.125, ((0, 64), (1, 16)))
    w_down = centred(arg_keys[7], (N_NODE, HALF, D), (4 * D) ** -0.5, 0.03125, ((0, 64), (2, 16)))
    return {"grad_out": grad_out, "route_expert": route_expert, "gate_prob": gate_prob, "saved_gate": saved_gate, "saved_up": saved_up, "w_gate": w_gate, "w_up": w_up, "w_down": w_down}


FULL_PRECISION = lax.Precision.HIGHEST


def slot_table(routes, experts, capacity):
    tokens = routes.shape[0]
    labels = jnp.arange(experts, dtype=jnp.int32)
    named = routes[:, :, None] == labels[None, None, :]
    onehot = jnp.sum(named.astype(jnp.float32), axis=1)
    positions = jnp.arange(tokens, dtype=jnp.int32)
    earlier_mask = (positions[:, None] > positions[None, :]).astype(jnp.float32)
    before = jnp.dot(earlier_mask, onehot, precision=FULL_PRECISION)
    picked = jnp.sum(jnp.where(named, before[:, None, :], 0.0), axis=2)
    slot_index = routes * capacity + picked.astype(jnp.int32)
    places = jnp.arange(experts * capacity, dtype=jnp.int32)
    return slot_index[None, :, :] == places[:, None, None]


def unit_grads(grad_units, gate_saved, up_saved):
    gate_value = gate_saved.astype(jnp.float32)
    up_value = up_saved.astype(jnp.float32)
    sigmoid_gate = jax.nn.sigmoid(gate_value)
    activation = gate_value * sigmoid_gate
    prob_part = jnp.sum(activation * up_value * grad_units, axis=0)
    grad_gate = (grad_units * up_value * sigmoid_gate * (1.0 + gate_value * (1.0 - sigmoid_gate))).astype(jnp.bfloat16)
    grad_upper = (grad_units * activation).astype(jnp.bfloat16)
    return grad_gate, grad_upper, prob_part


def expert_grads(token_rows, gate_saved, up_saved, gate_weight, up_weight, down_weight):
    slot_count = token_rows.shape[0]
    split_rows = token_rows.astype(jnp.float32).reshape(slot_count, N_LOCAL, FEAT)
    split_down = down_weight.astype(jnp.float32).reshape(HALF, N_LOCAL, FEAT)
    partials = jnp.einsum("fjd,sjd->jfs", split_down, split_rows)
    rounded = lax.optimization_barrier(partials.astype(jnp.bfloat16))
    grad_units = jnp.sum(rounded.astype(jnp.float32), axis=0)
    grad_gate, grad_upper, prob_part = unit_grads(grad_units, gate_saved, up_saved)
    route_grad = jnp.dot(gate_weight, grad_gate, preferred_element_type=jnp.float32)
    route_grad = route_grad + jnp.dot(up_weight, grad_upper, preferred_element_type=jnp.float32)
    return route_grad.astype(jnp.bfloat16), prob_part.astype(jnp.bfloat16)


def reference(grad_out, route_expert, gate_prob, saved_gate, saved_up, w_gate, w_up, w_down):
    node_rows = grad_out.reshape(N_NODE, TOK_NODE, D)
    node_routes = route_expert.reshape(N_NODE, TOK_NODE, TOPK)
    node_probs = gate_prob.reshape(N_NODE, TOK_NODE, TOPK)

    def outgoing_rows(operands):
        routes, token_rows = operands
        slot_match = slot_table(routes, EXPERTS, CAP)
        dispatch_mask = jnp.any(slot_match, axis=2).astype(jnp.bfloat16)
        return jnp.dot(dispatch_mask, token_rows, preferred_element_type=jnp.float32).astype(jnp.bfloat16)

    buffers = lax.map(outgoing_rows, (node_routes, node_rows))
    by_expert = buffers.reshape(N_NODE, EXPERTS, CAP, D).transpose(1, 0, 2, 3).reshape(EXPERTS, SLOTS, D)

    def per_half(operands):
        index, gate_saved, up_saved, gate_weight, up_weight, down_weight = operands
        token_rows = lax.dynamic_index_in_dim(by_expert, index // 2, 0, keepdims=False)
        return expert_grads(token_rows, gate_saved, up_saved, gate_weight, up_weight, down_weight)

    half_ids = jnp.arange(N_NODE, dtype=jnp.int32)
    route_halves, prob_halves = lax.map(per_half, (half_ids, saved_gate, saved_up, w_gate, w_up, w_down))
    back_rows = route_halves.reshape(N_NODE, D, N_NODE, CAP).transpose(2, 0, 3, 1)
    back_rows = jnp.sum(back_rows.astype(jnp.float32).reshape(N_NODE, EXPERTS, 2, CAP, D), axis=2).reshape(N_NODE, EXPERTS * CAP, D)
    back_probs = prob_halves.reshape(N_NODE, N_NODE, CAP).transpose(1, 0, 2)
    back_probs = jnp.sum(back_probs.astype(jnp.float32).reshape(N_NODE, EXPERTS, 2, CAP), axis=2).reshape(N_NODE, EXPERTS * CAP)

    def combine(operands):
        routes, probs, rows_back, probs_back = operands
        slot_match = slot_table(routes, EXPERTS, CAP)
        weights = jnp.sum(jnp.where(slot_match, probs[None, :, :], 0.0), axis=2)
        grad_rows = lax.dot_general(weights, rows_back, (((0,), (0,)), ((), ())), precision=FULL_PRECISION)
        grad_probs = jnp.sum(jnp.where(slot_match, probs_back[:, None, None], 0.0), axis=0)
        return grad_rows.astype(jnp.bfloat16), grad_probs.astype(jnp.bfloat16)

    grad_rows, grad_probs = lax.map(combine, (node_routes, node_probs, back_rows, back_probs))
    return grad_rows.reshape(TOKENS, D), grad_probs.reshape(TOKENS, TOPK)
```

```python
import jax
import jax.numpy as jnp
from jax import lax
from jax.sharding import Mesh
from jax.sharding import PartitionSpec as P

FULL_PRECISION = lax.Precision.HIGHEST
NODE = ("z", "y")


def slot_table(routes, experts, capacity):
    tokens = routes.shape[0]
    labels = jnp.arange(experts, dtype=jnp.int32)
    named = routes[:, :, None] == labels[None, None, :]
    onehot = jnp.sum(named.astype(jnp.float32), axis=1)
    positions = jnp.arange(tokens, dtype=jnp.int32)
    earlier_mask = (positions[:, None] > positions[None, :]).astype(jnp.float32)
    before = jnp.dot(earlier_mask, onehot, precision=FULL_PRECISION)
    picked = jnp.sum(jnp.where(named, before[:, None, :], 0.0), axis=2)
    slot_index = routes * capacity + picked.astype(jnp.int32)
    places = jnp.arange(experts * capacity, dtype=jnp.int32)
    return slot_index[None, :, :] == places[:, None, None]


def unit_grads(grad_units, gate_saved, up_saved):
    gate_value = gate_saved.astype(jnp.float32)
    up_value = up_saved.astype(jnp.float32)
    sigmoid_gate = jax.nn.sigmoid(gate_value)
    activation = gate_value * sigmoid_gate
    prob_part = jnp.sum(activation * up_value * grad_units, axis=0)
    grad_gate = (
        grad_units * up_value * sigmoid_gate * (1.0 + gate_value * (1.0 - sigmoid_gate))
    ).astype(jnp.bfloat16)
    grad_upper = (grad_units * activation).astype(jnp.bfloat16)
    return (grad_gate, grad_upper, prob_part)


def shards(grad_out, route_expert, gate_prob, saved_gate, saved_up, w_gate, w_up, w_down):
    groups = lax.axis_size(NODE)
    experts = groups // 2
    slots_all = saved_gate.shape[2]
    capacity = slots_all // groups
    feat_width = grad_out.shape[1]
    block_rows = capacity * feat_width // 128
    slot_match = slot_table(route_expert, experts, capacity)
    dispatch_mask = jnp.any(slot_match, axis=2).astype(jnp.bfloat16)
    outgoing = jnp.dot(dispatch_mask, grad_out, preferred_element_type=jnp.float32).astype(
        jnp.bfloat16
    )
    outgoing = jnp.repeat(outgoing.reshape(experts, block_rows, 128), 2, axis=0)
    arrived = lax.all_to_all(outgoing, NODE, split_axis=0, concat_axis=0, tiled=True)
    arrived = arrived.reshape(slots_all, feat_width)
    partial = lax.dot_general(
        w_down[0], arrived, (((1,), (1,)), ((), ())), preferred_element_type=jnp.float32
    ).astype(jnp.bfloat16)
    halves = lax.psum_scatter(partial, "c", scatter_dimension=0, tiled=True)
    halves = lax.psum(halves, "x")
    grad_units = lax.all_gather(halves, "c", axis=0, tiled=True).astype(jnp.float32)
    grad_gate, grad_upper, prob_grad = unit_grads(grad_units, saved_gate[0], saved_up[0])
    route_grad = jnp.dot(w_gate[0], grad_gate, preferred_element_type=jnp.float32) + jnp.dot(
        w_up[0], grad_upper, preferred_element_type=jnp.float32
    )
    packed = route_grad.astype(jnp.bfloat16).T.reshape(groups, block_rows, 128)
    probs = jnp.pad(
        prob_grad.astype(jnp.bfloat16).reshape(groups, 1, capacity),
        ((0, 0), (0, 0), (0, 128 - capacity)),
    )
    returned = lax.all_to_all(
        jnp.concatenate([packed, probs], axis=1), NODE, split_axis=0, concat_axis=0, tiled=True
    )
    rows = returned[:, :block_rows].reshape(experts, 2, capacity, feat_width)
    summed_rows = jnp.sum(rows.astype(jnp.float32), axis=1).reshape(
        experts * capacity, feat_width
    )
    prob_rows = returned[:, block_rows, :capacity].reshape(experts, 2, capacity)
    summed_probs = jnp.sum(prob_rows.astype(jnp.float32), axis=1).reshape(experts * capacity)
    weights = jnp.sum(jnp.where(slot_match, gate_prob[None, :, :], 0.0), axis=2)
    grad_in = lax.dot_general(
        weights, summed_rows, (((0,), (0,)), ((), ())), precision=FULL_PRECISION
    )
    grad_prob = jnp.sum(jnp.where(slot_match, summed_probs[:, None, None], 0.0), axis=0)
    return (grad_in.astype(jnp.bfloat16), grad_prob.astype(jnp.bfloat16))


def solution(mesh):
    nodes, local = mesh.devices.shape
    rows = 8
    fine = Mesh(
        mesh.devices.reshape(nodes // rows, rows, local // 2, 2), ("z", "y", "x", "c")
    )
    node, feats = NODE, ("x", "c")
    return jax.shard_map(
        shards,
        mesh=fine,
        in_specs=(
            P(node, feats),
            P(node, None),
            P(node, None),
            P(node, None, None),
            P(node, None, None),
            P(node, feats, None),
            P(node, feats, None),
            P(node, None, feats),
        ),
        out_specs=(P(node, feats), P(node, None)),
        check_vma=False,
    )
```

```python
import jax
import jax.numpy as jnp
from jax import lax
from jax.sharding import Mesh
from jax.sharding import PartitionSpec as P

FULL_PRECISION = lax.Precision.HIGHEST
PAIR = ("z", "yh")


def slot_table(routes, experts, capacity):
    tokens = routes.shape[0]
    labels = jnp.arange(experts, dtype=jnp.int32)
    named = routes[:, :, None] == labels[None, None, :]
    onehot = jnp.sum(named.astype(jnp.float32), axis=1)
    positions = jnp.arange(tokens, dtype=jnp.int32)
    earlier_mask = (positions[:, None] > positions[None, :]).astype(jnp.float32)
    before = jnp.dot(earlier_mask, onehot, precision=FULL_PRECISION)
    picked = jnp.sum(jnp.where(named, before[:, None, :], 0.0), axis=2)
    slot_index = routes * capacity + picked.astype(jnp.int32)
    places = jnp.arange(experts * capacity, dtype=jnp.int32)
    return slot_index[None, :, :] == places[:, None, None]


def unit_grads(grad_units, gate_saved, up_saved):
    gate_value = gate_saved.astype(jnp.float32)
    up_value = up_saved.astype(jnp.float32)
    sigmoid_gate = jax.nn.sigmoid(gate_value)
    activation = gate_value * sigmoid_gate
    prob_part = jnp.sum(activation * up_value * grad_units, axis=0)
    grad_gate = (
        grad_units * up_value * sigmoid_gate * (1.0 + gate_value * (1.0 - sigmoid_gate))
    ).astype(jnp.bfloat16)
    grad_upper = (grad_units * activation).astype(jnp.bfloat16)
    return (grad_gate, grad_upper, prob_part)


def swap(value, axis):
    return lax.ppermute(value, axis, ((0, 1), (1, 0)))


def shards(grad_out, route_expert, gate_prob, saved_gate, saved_up, w_gate, w_up, w_down):
    experts = lax.axis_size(PAIR)
    slots_all = saved_gate.shape[2]
    hidden = saved_gate.shape[1]
    capacity = slots_all // (2 * experts)
    feat_width = grad_out.shape[1]
    block_rows = capacity * feat_width // 128
    chips = lax.axis_size("x")
    core = lax.axis_index("c")
    side = lax.axis_index("yl")
    slot_match = slot_table(route_expert, experts, capacity)
    dispatch_mask = jnp.any(slot_match, axis=2).astype(jnp.bfloat16)
    outgoing = jnp.dot(dispatch_mask, grad_out, preferred_element_type=jnp.float32).astype(
        jnp.bfloat16
    )
    outgoing = outgoing.reshape(experts, block_rows, 128)
    own_rows = lax.all_to_all(outgoing, PAIR, split_axis=0, concat_axis=0, tiled=True)
    pair_rows = swap(own_rows, "yl")
    first = jnp.where(side == 0, own_rows, pair_rows)
    second = jnp.where(side == 0, pair_rows, own_rows)
    arrived = jnp.stack([first, second], axis=1).reshape(slots_all, feat_width)
    partial = lax.dot_general(
        w_down[0], arrived, (((1,), (1,)), ((), ())), preferred_element_type=jnp.float32
    ).astype(jnp.bfloat16)
    half = hidden // 2
    kept = lax.dynamic_slice_in_dim(partial, core * half, half, 0)
    other = swap(lax.dynamic_slice_in_dim(partial, (1 - core) * half, half, 0), "c")
    on_chip = (kept.astype(jnp.float32) + other.astype(jnp.float32)).astype(jnp.bfloat16)
    pieces = lax.all_to_all(
        on_chip.reshape(chips, half // chips, slots_all), "x", split_axis=0, concat_axis=0, tiled=True
    )
    summed = jnp.sum(pieces.astype(jnp.float32), axis=0).astype(jnp.bfloat16)
    spread = lax.all_to_all(
        jnp.broadcast_to(summed[None], pieces.shape), "x", split_axis=0, concat_axis=0, tiled=True
    ).reshape(half, slots_all)
    partner = swap(spread, "c")
    grad_units = jnp.concatenate(
        [jnp.where(core == 0, spread, partner), jnp.where(core == 0, partner, spread)], axis=0
    ).astype(jnp.float32)
    grad_gate, grad_upper, prob_grad = unit_grads(grad_units, saved_gate[0], saved_up[0])
    route_grad = jnp.dot(w_gate[0], grad_gate, preferred_element_type=jnp.float32) + jnp.dot(
        w_up[0], grad_upper, preferred_element_type=jnp.float32
    )
    packed = route_grad.astype(jnp.bfloat16).T.reshape(experts, 2, block_rows, 128)
    probs = jnp.pad(
        prob_grad.astype(jnp.bfloat16).reshape(experts, 2, 1, capacity),
        ((0, 0), (0, 0), (0, 0), (0, 128 - capacity)),
    )
    packed = jnp.concatenate([packed, probs], axis=2)
    kept_back = jnp.where(side == 0, packed[:, 0], packed[:, 1])
    pair_back = swap(jnp.where(side == 0, packed[:, 1], packed[:, 0]), "yl")
    both = (kept_back.astype(jnp.float32) + pair_back.astype(jnp.float32)).astype(jnp.bfloat16)
    returned = lax.all_to_all(both, PAIR, split_axis=0, concat_axis=0, tiled=True)
    summed_rows = returned[:, :block_rows].reshape(experts * capacity, feat_width)
    summed_probs = returned[:, block_rows, :capacity].reshape(experts * capacity)
    weights = jnp.sum(jnp.where(slot_match, gate_prob[None, :, :], 0.0), axis=2)
    grad_in = lax.dot_general(
        weights,
        summed_rows.astype(jnp.float32),
        (((0,), (0,)), ((), ())),
        precision=FULL_PRECISION,
    )
    grad_prob = jnp.sum(
        jnp.where(slot_match, summed_probs.astype(jnp.float32)[:, None, None], 0.0), axis=0
    )
    return (grad_in.astype(jnp.bfloat16), grad_prob.astype(jnp.bfloat16))


def solution(mesh):
    nodes, local = mesh.devices.shape
    rows = 8
    fine = Mesh(
        mesh.devices.reshape(nodes // rows, rows // 2, 2, local // 2, 2),
        ("z", "yh", "yl", "x", "c"),
    )
    node, feats = ("z", "yh", "yl"), ("x", "c")
    return jax.shard_map(
        shards,
        mesh=fine,
        in_specs=(
            P(node, feats),
            P(node, None),
            P(node, None),
            P(node, None, None),
            P(node, None, None),
            P(node, feats, None),
            P(node, feats, None),
            P(node, None, feats),
        ),
        out_specs=(P(node, feats), P(node, None)),
        check_vma=False,
    )
```

```python
import jax
import jax.numpy as jnp
from jax import lax
from jax.sharding import Mesh
from jax.sharding import PartitionSpec as P

FULL_PRECISION = lax.Precision.HIGHEST
PAIR = ("z", "yh")


def slot_table(routes, experts, capacity):
    tokens = routes.shape[0]
    labels = jnp.arange(experts, dtype=jnp.int32)
    named = routes[:, :, None] == labels[None, None, :]
    onehot = jnp.sum(named.astype(jnp.float32), axis=1)
    positions = jnp.arange(tokens, dtype=jnp.int32)
    earlier_mask = (positions[:, None] > positions[None, :]).astype(jnp.float32)
    before = jnp.dot(earlier_mask, onehot, precision=FULL_PRECISION)
    picked = jnp.sum(jnp.where(named, before[:, None, :], 0.0), axis=2)
    slot_index = routes * capacity + picked.astype(jnp.int32)
    places = jnp.arange(experts * capacity, dtype=jnp.int32)
    return slot_index[None, :, :] == places[:, None, None]


def unit_grads(grad_units, gate_saved, up_saved):
    gate_value = gate_saved.astype(jnp.float32)
    up_value = up_saved.astype(jnp.float32)
    sigmoid_gate = jax.nn.sigmoid(gate_value)
    activation = gate_value * sigmoid_gate
    prob_part = jnp.sum(activation * up_value * grad_units, axis=1)
    grad_gate = (
        grad_units * up_value * sigmoid_gate * (1.0 + gate_value * (1.0 - sigmoid_gate))
    ).astype(jnp.bfloat16)
    grad_upper = (grad_units * activation).astype(jnp.bfloat16)
    return (grad_gate, grad_upper, prob_part)


def swap(value, axis):
    return lax.ppermute(value, axis, ((0, 1), (1, 0)))


def times_transposed(left, right):
    return lax.dot_general(
        left, right, (((1,), (1,)), ((), ())), preferred_element_type=jnp.float32
    )


def chip_sum(rows, down, core):
    partial = times_transposed(rows, down).astype(jnp.bfloat16)
    half = partial.shape[1] // 2
    kept = lax.dynamic_slice_in_dim(partial, core * half, half, 1)
    other = swap(lax.dynamic_slice_in_dim(partial, (1 - core) * half, half, 1), "c")
    return (kept.astype(jnp.float32) + other.astype(jnp.float32)).astype(jnp.bfloat16)


def over_x(blocks):
    return lax.all_to_all(blocks, "x", split_axis=0, concat_axis=0, tiled=True)


def to_sum(on_chip):
    chips = lax.axis_size("x")
    return over_x(on_chip.reshape(chips, on_chip.shape[0] // chips, -1))


def add_up(pieces):
    return jnp.sum(pieces.astype(jnp.float32), axis=0).astype(jnp.bfloat16)


def spread(piece):
    chips = lax.axis_size("x")
    return over_x(jnp.broadcast_to(piece[None], (chips, *piece.shape))).reshape(
        chips * piece.shape[0], -1
    )


def chip_gather(spread_half, core):
    partner = swap(spread_half, "c")
    return jnp.concatenate(
        [
            jnp.where(core == 0, spread_half, partner),
            jnp.where(core == 0, partner, spread_half),
        ],
        axis=1,
    )


def routes_back(grad_units, gate_saved, up_saved, gate_weight, up_weight, experts, capacity):
    grad_gate, grad_upper, prob_grad = unit_grads(
        grad_units.astype(jnp.float32), gate_saved, up_saved
    )
    route_grad = times_transposed(grad_gate, gate_weight) + times_transposed(
        grad_upper, up_weight
    )
    packed = route_grad.astype(jnp.bfloat16).reshape(experts, -1, 128)
    probs = jnp.pad(
        prob_grad.astype(jnp.bfloat16).reshape(experts, 1, capacity),
        ((0, 0), (0, 0), (0, 128 - capacity)),
    )
    return jnp.concatenate([packed, probs], axis=1)


def shards(grad_out, route_expert, gate_prob, saved_gate, saved_up, w_gate, w_up, w_down):
    experts = lax.axis_size(PAIR)
    slots_all = saved_gate.shape[2]
    slots_side = slots_all // 2
    capacity = slots_side // experts
    feat_width = grad_out.shape[1]
    block_rows = capacity * feat_width // 128
    core = lax.axis_index("c")
    side = lax.axis_index("yl")
    slot_match = slot_table(route_expert, experts, capacity)
    dispatch_mask = jnp.any(slot_match, axis=2).astype(jnp.bfloat16)
    outgoing = jnp.dot(dispatch_mask, grad_out, preferred_element_type=jnp.float32).astype(
        jnp.bfloat16
    )
    outgoing = outgoing.reshape(experts, block_rows, 128)
    own_rows = lax.all_to_all(outgoing, PAIR, split_axis=0, concat_axis=0, tiled=True)
    pair_rows = swap(own_rows, "yl")
    row = jnp.arange(slots_side, dtype=jnp.int32)[:, None]
    place = jnp.arange(slots_all, dtype=jnp.int32)[None, :]

    def picked(saved, which):
        source = (row // capacity * 2 + which) * capacity + row % capacity
        pick = (place == source).astype(jnp.bfloat16)
        return times_transposed(pick, saved).astype(jnp.bfloat16)

    own_chip = chip_sum(own_rows.reshape(slots_side, feat_width), w_down[0], core)
    own_pieces = to_sum(own_chip)
    pair_chip = chip_sum(pair_rows.reshape(slots_side, feat_width), w_down[0], core)
    pair_chip, own_pieces = lax.optimization_barrier((pair_chip, own_pieces))
    pair_pieces = to_sum(pair_chip)
    pair_half = spread(add_up(pair_pieces))
    own_piece, pair_half = lax.optimization_barrier((add_up(own_pieces), pair_half))
    own_half = spread(own_piece)
    pair_routes = routes_back(
        chip_gather(pair_half, core),
        picked(saved_gate[0], 1 - side),
        picked(saved_up[0], 1 - side),
        w_gate[0],
        w_up[0],
        experts,
        capacity,
    )
    pair_back = swap(pair_routes, "yl")
    own_half, _ = lax.optimization_barrier((own_half, pair_routes))
    own_routes = routes_back(
        chip_gather(own_half, core),
        picked(saved_gate[0], side),
        picked(saved_up[0], side),
        w_gate[0],
        w_up[0],
        experts,
        capacity,
    )
    both = (own_routes.astype(jnp.float32) + pair_back.astype(jnp.float32)).astype(jnp.bfloat16)
    returned = lax.all_to_all(both, PAIR, split_axis=0, concat_axis=0, tiled=True)
    summed_rows = returned[:, :block_rows].reshape(experts * capacity, feat_width)
    summed_probs = returned[:, block_rows, :capacity].reshape(experts * capacity)
    weights = jnp.sum(jnp.where(slot_match, gate_prob[None, :, :], 0.0), axis=2)
    grad_in = lax.dot_general(
        weights,
        summed_rows.astype(jnp.float32),
        (((0,), (0,)), ((), ())),
        precision=FULL_PRECISION,
    )
    grad_prob = jnp.sum(
        jnp.where(slot_match, summed_probs.astype(jnp.float32)[:, None, None], 0.0), axis=0
    )
    return (grad_in.astype(jnp.bfloat16), grad_prob.astype(jnp.bfloat16))


def solution(mesh):
    nodes, local = mesh.devices.shape
    rows = 8
    fine = Mesh(
        mesh.devices.reshape(nodes // rows, rows // 2, 2, local // 2, 2),
        ("z", "yh", "yl", "x", "c"),
    )
    node, feats = ("z", "yh", "yl"), ("x", "c")
    return jax.shard_map(
        shards,
        mesh=fine,
        in_specs=(
            P(node, feats),
            P(node, None),
            P(node, None),
            P(node, None, None),
            P(node, None, None),
            P(node, feats, None),
            P(node, feats, None),
            P(node, None, feats),
        ),
        out_specs=(P(node, feats), P(node, None)),
        check_vma=False,
    )
```

```python
import jax
import jax.numpy as jnp
from jax import lax
from jax.sharding import Mesh
from jax.sharding import PartitionSpec as P

FULL_PRECISION = lax.Precision.HIGHEST
PAIR = ("z", "yh")
NODE = ("z", "yh", "yl")


def slot_table(routes, experts, capacity):
    tokens = routes.shape[0]
    labels = jnp.arange(experts, dtype=jnp.int32)
    named = routes[:, :, None] == labels[None, None, :]
    onehot = jnp.sum(named.astype(jnp.float32), axis=1)
    positions = jnp.arange(tokens, dtype=jnp.int32)
    earlier_mask = (positions[:, None] > positions[None, :]).astype(jnp.float32)
    before = jnp.dot(earlier_mask, onehot, precision=FULL_PRECISION)
    picked = jnp.sum(jnp.where(named, before[:, None, :], 0.0), axis=2)
    slot_index = routes * capacity + picked.astype(jnp.int32)
    places = jnp.arange(experts * capacity, dtype=jnp.int32)
    return slot_index[None, :, :] == places[:, None, None]


def unit_grads(grad_units, gate_saved, up_saved):
    gate_value = gate_saved.astype(jnp.float32)
    up_value = up_saved.astype(jnp.float32)
    sigmoid_gate = jax.nn.sigmoid(gate_value)
    activation = gate_value * sigmoid_gate
    prob_part = jnp.sum(activation * up_value * grad_units, axis=1)
    grad_gate = (
        grad_units * up_value * sigmoid_gate * (1.0 + gate_value * (1.0 - sigmoid_gate))
    ).astype(jnp.bfloat16)
    grad_upper = (grad_units * activation).astype(jnp.bfloat16)
    return (grad_gate, grad_upper, prob_part)


def swap(value, axis):
    return lax.ppermute(value, axis, ((0, 1), (1, 0)))


def times_transposed(left, right):
    return lax.dot_general(
        left, right, (((1,), (1,)), ((), ())), preferred_element_type=jnp.float32
    )


def over_x(blocks):
    return lax.all_to_all(blocks, "x", split_axis=0, concat_axis=0, tiled=True)


def add_up(pieces):
    return jnp.sum(pieces.astype(jnp.float32), axis=0).astype(jnp.bfloat16)


def spread(piece):
    chips = lax.axis_size("x")
    return over_x(jnp.broadcast_to(piece[None], (chips, *piece.shape))).reshape(
        chips * piece.shape[0], -1
    )


def chip_gather(half, core):
    partner = swap(half, "c")
    return jnp.concatenate(
        [jnp.where(core == 0, half, partner), jnp.where(core == 0, partner, half)], axis=1
    )


def routes_back(grad_units, gate_saved, up_saved, gate_weight, up_weight, experts, capacity):
    grad_gate, grad_upper, prob_grad = unit_grads(
        grad_units.astype(jnp.float32), gate_saved, up_saved
    )
    route_grad = times_transposed(grad_gate, gate_weight) + times_transposed(
        grad_upper, up_weight
    )
    packed = route_grad.astype(jnp.bfloat16).reshape(experts, -1, 128)
    probs = jnp.pad(
        prob_grad.astype(jnp.bfloat16).reshape(experts, 1, capacity),
        ((0, 0), (0, 0), (0, 128 - capacity)),
    )
    return jnp.concatenate([packed, probs], axis=1)


def turned(pair):
    return (pair % lax.axis_size("yh")) // (lax.axis_size("yh") // 2)


def over_group(blocks):
    pairs = lax.axis_size(PAIR)
    groups = [[2 * p + (g ^ turned(p)) for p in range(pairs)] for g in range(2)]
    return lax.all_to_all(
        blocks, NODE, split_axis=0, concat_axis=0, tiled=True, axis_index_groups=groups
    )


def shards(grad_out, route_expert, gate_prob, saved_gate, saved_up, w_gate, w_up, w_down):
    experts = lax.axis_size(PAIR)
    chips = lax.axis_size("x")
    slots_all = saved_gate.shape[2]
    slots_side = slots_all // 2
    capacity = slots_side // experts
    feat_width = grad_out.shape[1]
    half = saved_gate.shape[1] // 2
    block_rows = capacity * feat_width // 128
    core = lax.axis_index("c")
    group = lax.axis_index("yl") ^ turned(lax.axis_index("yh"))
    slot_match = slot_table(route_expert, experts, capacity)
    dispatch_mask = jnp.any(slot_match, axis=2).astype(jnp.bfloat16)
    outgoing = jnp.dot(dispatch_mask, grad_out, preferred_element_type=jnp.float32).astype(
        jnp.bfloat16
    )
    own_rows = over_group(outgoing.reshape(experts, block_rows, 128))

    slot = jnp.arange(slots_all, dtype=jnp.int32)[:, None]
    place = jnp.arange(slots_all, dtype=jnp.int32)[None, :]
    pair = slot // capacity % experts
    member = group ^ turned(pair) ^ (slot // slots_side)
    source = (2 * pair + member) * capacity + slot % capacity
    order = (place == source).astype(jnp.bfloat16)
    gate_rows = times_transposed(order, saved_gate[0]).astype(jnp.bfloat16)
    up_rows = times_transposed(order, saved_up[0]).astype(jnp.bfloat16)
    down_kept = lax.dynamic_slice_in_dim(w_down[0], core * half, half, 0)
    down_other = swap(lax.dynamic_slice_in_dim(w_down[0], (1 - core) * half, half, 0), "c")
    own_rows, gate_rows, up_rows, down_other = lax.optimization_barrier(
        (own_rows, gate_rows, up_rows, down_other)
    )

    pair_rows = swap(own_rows, "yl")
    own_other = swap(own_rows, "c")
    pair_rows, own_other = lax.optimization_barrier((pair_rows, own_other))
    pair_other = swap(pair_rows, "c")
    kept_rows = jnp.concatenate([own_rows, pair_rows]).reshape(slots_all, feat_width)
    other_rows = jnp.concatenate([own_other, pair_other]).reshape(slots_all, feat_width)
    on_chip = (
        times_transposed(kept_rows, down_kept) + times_transposed(other_rows, down_other)
    ).astype(jnp.bfloat16)
    pieces = over_x(on_chip.reshape(chips, slots_all // chips, half))
    half_units = spread(add_up(pieces))
    pair_routes = routes_back(
        chip_gather(half_units[slots_side:], core),
        gate_rows[slots_side:],
        up_rows[slots_side:],
        w_gate[0],
        w_up[0],
        experts,
        capacity,
    )
    pair_back = swap(pair_routes, "yl")
    own_units, _ = lax.optimization_barrier((chip_gather(half_units[:slots_side], core), pair_routes))
    own_routes = routes_back(
        own_units,
        gate_rows[:slots_side],
        up_rows[:slots_side],
        w_gate[0],
        w_up[0],
        experts,
        capacity,
    )
    both = (own_routes.astype(jnp.float32) + pair_back.astype(jnp.float32)).astype(jnp.bfloat16)
    returned = over_group(both)
    summed_rows = returned[:, :block_rows].reshape(experts * capacity, feat_width)
    summed_probs = returned[:, block_rows, :capacity].reshape(experts * capacity)
    weights = jnp.sum(jnp.where(slot_match, gate_prob[None, :, :], 0.0), axis=2)
    grad_in = lax.dot_general(
        weights,
        summed_rows.astype(jnp.float32),
        (((0,), (0,)), ((), ())),
        precision=FULL_PRECISION,
    )
    grad_prob = jnp.sum(
        jnp.where(slot_match, summed_probs.astype(jnp.float32)[:, None, None], 0.0), axis=0
    )
    return (grad_in.astype(jnp.bfloat16), grad_prob.astype(jnp.bfloat16))


def solution(mesh):
    nodes, local = mesh.devices.shape
    rows = 8
    fine = Mesh(
        mesh.devices.reshape(nodes // rows, rows // 2, 2, local // 2, 2),
        ("z", "yh", "yl", "x", "c"),
    )
    node, feats = NODE, ("x", "c")
    return jax.shard_map(
        shards,
        mesh=fine,
        in_specs=(
            P(node, feats),
            P(node, None),
            P(node, None),
            P(node, None, None),
            P(node, None, None),
            P(node, feats, None),
            P(node, feats, None),
            P(node, None, feats),
        ),
        out_specs=(P(node, feats), P(node, None)),
        check_vma=False,
    )
```

```python
import functools

import jax
import jax.numpy as jnp
import numpy as np
from jax import lax
from jax.experimental import pallas as pl
from jax.experimental.pallas import tpu as pltpu
from jax.sharding import Mesh
from jax.sharding import PartitionSpec as P

PAIR = ("z", "yh")
NODE = ("z", "yh", "yl")
LANES = 128
PACKED = 40
BATCH = 8


def swap(value, axis):
    return lax.ppermute(value, axis, ((0, 1), (1, 0)))


def times_transposed(left, right):
    return lax.dot_general(
        left, right, (((1,), (1,)), ((), ())), preferred_element_type=jnp.float32
    )


def over_x(blocks):
    return lax.all_to_all(blocks, "x", split_axis=0, concat_axis=0, tiled=True)


def turned(pair):
    return (pair % lax.axis_size("yh")) // (lax.axis_size("yh") // 2)


def over_group(blocks):
    pairs = lax.axis_size(PAIR)
    groups = [[2 * p + (g ^ turned(p)) for p in range(pairs)] for g in range(2)]
    return lax.all_to_all(
        blocks, NODE, split_axis=0, concat_axis=0, tiled=True, axis_index_groups=groups
    )


def packing(capacity):
    kinds = np.zeros((5, BATCH, capacity, BATCH, PACKED), np.float32)
    for block in range(BATCH):
        for slot in range(capacity):
            for kind in range(3):
                kinds[kind, block, slot, block, capacity * kind + slot] = 1
            kinds[3, block, slot, block, 3 * capacity + slot % (capacity // 2)] = 1
            kinds[4, block, slot, block, 3 * capacity + capacity // 2] = 1
    return kinds.reshape(5, BATCH * capacity, BATCH * PACKED)


def tail_lanes(rank, capacity):
    lane = lax.broadcasted_iota(jnp.int32, (rank.shape[0], LANES), 1)
    return (lane < LANES // 2) == (rank < capacity // 2)


def unpacked(block_ref, pick_ref, rank, capacity):
    span = BATCH * capacity
    features, probs = [], []
    for batch in range(block_ref.shape[0] // BATCH):
        rows = block_ref[batch * BATCH : (batch + 1) * BATCH].astype(jnp.float32)
        rows = rows.reshape(BATCH * PACKED, LANES).astype(jnp.bfloat16)
        picked = jnp.dot(pick_ref[...], rows, preferred_element_type=jnp.float32)
        own = rank[batch * span : (batch + 1) * span]
        tail = jnp.where(tail_lanes(own, capacity), picked[3 * span : 4 * span], 0.0)
        groups = [picked[k * span : (k + 1) * span] for k in range(3)] + [tail]
        features.append(jnp.concatenate(groups, axis=1).astype(jnp.bfloat16))
        if picked.shape[0] > 4 * span:
            lane = lax.broadcasted_iota(jnp.int32, (span, LANES), 1)
            prob = jnp.where(lane == own, picked[4 * span :], 0.0)
            probs.append(jnp.sum(prob, axis=1, keepdims=True))
    return features, probs


def pack(rows, probs, put_ref, rank, out_ref, capacity):
    span = BATCH * capacity
    for batch in range(out_ref.shape[0] // BATCH):
        own = rank[batch * span : (batch + 1) * span]
        part = rows[batch * span : (batch + 1) * span]
        tail = part[:, 3 * LANES :]
        tail = jnp.where(
            tail_lanes(own, capacity), jnp.concatenate([tail, tail], axis=1), 0.0
        )
        groups = [part[:, k * LANES : (k + 1) * LANES] for k in range(3)] + [tail]
        if probs is not None:
            lane = lax.broadcasted_iota(jnp.int32, (span, LANES), 1)
            groups.append(jnp.where(lane == own, probs[batch * span : (batch + 1) * span], 0.0))
        stacked = jnp.concatenate(groups, axis=0).astype(jnp.bfloat16)
        packed = jnp.dot(
            put_ref[:, : stacked.shape[0]], stacked, preferred_element_type=jnp.float32
        )
        out_ref[batch * BATCH : (batch + 1) * BATCH] = packed.reshape(
            BATCH, PACKED, LANES
        ).astype(jnp.bfloat16)


def slot_masks(routes, widen, expert, rank):
    experts = widen.shape[1]
    tokens = routes.shape[1]
    label = lax.broadcasted_iota(jnp.int32, (experts, tokens), 0)
    named = (routes[0:1] == label) | (routes[1:2] == label)
    earlier = lax.broadcasted_iota(jnp.int32, (tokens, tokens), 0) < lax.broadcasted_iota(
        jnp.int32, (tokens, tokens), 1
    )
    ones = jnp.where(named, 1.0, 0.0).astype(jnp.bfloat16)
    before = jnp.dot(
        ones, jnp.where(earlier, 1.0, 0.0).astype(jnp.bfloat16), preferred_element_type=jnp.float32
    )
    before = jnp.dot(widen, before.astype(jnp.bfloat16), preferred_element_type=jnp.float32)
    here = before == rank.astype(jnp.float32)
    return [here & (routes[k : k + 1] == expert) for k in range(2)]


def dispatch_kernel(capacity, routes_ref, grad_ref, widen_ref, expert_ref, rank_ref, put_ref, out_ref):
    first, second = slot_masks(routes_ref[...], widen_ref[...], expert_ref[...], rank_ref[...])
    mask = jnp.where(first | second, 1.0, 0.0).astype(jnp.bfloat16)
    rows = times_transposed(mask, grad_ref[...])
    pack(rows, None, put_ref, rank_ref[...], out_ref, capacity)


def down_kernel(
    capacity, core_ref, own_ref, own_far_ref, pair_ref, pair_far_ref, near_ref, far_ref, pick_ref, rank_ref, out_ref
):
    def stretched(weights):
        return jnp.concatenate([weights, weights[3 * LANES :]], axis=0)

    near, far = stretched(near_ref[...]), stretched(far_ref[...])
    span = BATCH * capacity
    done = 0
    for here_ref, there_ref in ((own_ref, own_far_ref), (pair_ref, pair_far_ref)):
        here, _ = unpacked(here_ref, pick_ref, rank_ref[...], capacity)
        there, _ = unpacked(there_ref, pick_ref, rank_ref[...], capacity)
        here, there = jnp.concatenate(here, axis=0), jnp.concatenate(there, axis=0)
        total = jnp.dot(here, near, preferred_element_type=jnp.float32)
        total = total + jnp.dot(there, far, preferred_element_type=jnp.float32)
        out_ref[done : done + total.shape[0]] = total.astype(jnp.bfloat16)
        done += total.shape[0]


def add_kernel(pieces_ref, out_ref):
    total = pieces_ref[0].astype(jnp.float32)
    for piece in range(1, pieces_ref.shape[0]):
        total = total + pieces_ref[piece].astype(jnp.float32)
    total = total.astype(jnp.bfloat16)
    for piece in range(out_ref.shape[0]):
        out_ref[piece] = total


def route_kernel(
    capacity,
    core_ref,
    near_ref,
    far_ref,
    gate_ref,
    up_ref,
    w_gate_ref,
    w_up_ref,
    put_ref,
    rank_ref,
    out_ref,
    total_ref,
    prob_ref,
):
    step = pl.program_id(0)

    @pl.when(step == 0)
    def _():
        total_ref[...] = jnp.zeros_like(total_ref)
        prob_ref[...] = jnp.zeros_like(prob_ref)

    units = jnp.where(step == 0, near_ref[...].astype(jnp.float32), far_ref[...].astype(jnp.float32))
    gate = gate_ref[...].astype(jnp.float32)
    up = up_ref[...].astype(jnp.float32)
    sigmoid = 1.0 / (1.0 + jnp.exp(-gate))
    upper = units * (gate * sigmoid)
    gates = units * up * sigmoid * (1.0 + gate * (1.0 - sigmoid))
    prob_ref[...] += jnp.sum(upper * up, axis=1, keepdims=True)
    total_ref[...] += times_transposed(
        gates.astype(jnp.bfloat16), w_gate_ref[...]
    ) + times_transposed(upper.astype(jnp.bfloat16), w_up_ref[...])

    @pl.when(step == 1)
    def _():
        pack(total_ref[...], prob_ref[...], put_ref, rank_ref[...], out_ref, capacity)


def sum_kernel(left_ref, right_ref, out_ref):
    out_ref[...] = (
        left_ref[...].astype(jnp.float32) + right_ref[...].astype(jnp.float32)
    ).astype(jnp.bfloat16)


def combine_kernel(
    capacity,
    back_ref,
    routes_ref,
    weight_ref,
    widen_ref,
    expert_ref,
    rank_ref,
    pick_ref,
    out_ref,
    prob_ref,
):
    masks = slot_masks(routes_ref[...], widen_ref[...], expert_ref[...], rank_ref[...])
    weights = jnp.where(masks[0], weight_ref[0:1], 0.0) + jnp.where(masks[1], weight_ref[1:2], 0.0)
    features, probs = unpacked(back_ref, pick_ref, rank_ref[...], capacity)
    wide = jnp.concatenate(features, axis=0)
    half = LANES // 2
    tail = wide[:, 3 * LANES : 3 * LANES + half] + wide[:, 3 * LANES + half :]
    rows = jnp.concatenate([wide[:, : 3 * LANES], tail], axis=1)
    total = jnp.zeros(out_ref.shape, jnp.float32)
    rest = weights
    for _ in range(3):
        part = rest.astype(jnp.bfloat16)
        rest = rest - part.astype(jnp.float32)
        total = total + lax.dot_general(
            rows, part, (((0,), (0,)), ((), ())), preferred_element_type=jnp.float32
        )
    out_ref[...] = total.astype(jnp.bfloat16)
    prob = jnp.concatenate(probs, axis=0)
    for k in range(2):
        prob_ref[k : k + 1] = jnp.sum(
            jnp.where(masks[k], prob, 0.0), axis=0, keepdims=True
        ).astype(jnp.bfloat16)


BIG = pltpu.CompilerParams(vmem_limit_bytes=40 * 1024 * 1024)
FULL = pltpu.CompilerParams(vmem_limit_bytes=60 * 1024 * 1024)


def whole(kernel, out_shape, *args, params=BIG):
    return pl.pallas_call(kernel, out_shape=out_shape, compiler_params=params)(*args)


def shards(grad_out, route_expert, gate_prob, saved_gate, saved_up, w_gate, w_up, w_down):
    experts = lax.axis_size(PAIR)
    chips = lax.axis_size("x")
    slots_all = saved_gate.shape[2]
    slots_side = slots_all // 2
    capacity = slots_side // experts
    feats = grad_out.shape[1]
    tokens = grad_out.shape[0]
    half = saved_gate.shape[1] // 2
    bf16 = jnp.bfloat16
    core = lax.axis_index("c")
    group = lax.axis_index("yl") ^ turned(lax.axis_index("yh"))
    numbers = np.arange(slots_side, dtype=np.int32)[:, None]
    expert_of = jnp.asarray(numbers // capacity)
    rank_of = jnp.asarray(numbers % capacity)
    widen = jnp.asarray(numbers // capacity == np.arange(experts)[None, :], bf16)
    kinds = packing(capacity)
    pick_all = jnp.asarray(kinds.reshape(-1, kinds.shape[2]), bf16)
    pick_rows = pick_all[: 4 * kinds.shape[1]]
    put_all = jnp.asarray(kinds.reshape(-1, kinds.shape[2]).T, bf16)
    block = jax.ShapeDtypeStruct((experts, PACKED, LANES), bf16)

    routes = route_expert.T
    outgoing = whole(
        functools.partial(dispatch_kernel, capacity),
        block,
        routes,
        grad_out.T,
        widen,
        expert_of,
        rank_of,
        put_all[:, : 4 * kinds.shape[1]],
        params=FULL,
    )
    own_rows = over_group(outgoing)

    slot = jnp.arange(slots_all, dtype=jnp.int32)[:, None]
    place = jnp.arange(slots_all, dtype=jnp.int32)[None, :]
    pair = slot // capacity % experts
    member = group ^ turned(pair) ^ (slot // slots_side)
    source = (2 * pair + member) * capacity + slot % capacity
    order = (place == source).astype(bf16)
    gate_rows = times_transposed(order, saved_gate[0]).astype(bf16)
    up_rows = times_transposed(order, saved_up[0]).astype(bf16)
    down = w_down[0].T
    down_far = swap(lax.dynamic_slice_in_dim(down, (1 - core) * half, half, 1), "c")
    own_rows, gate_rows, up_rows, down_far = lax.optimization_barrier(
        (own_rows, gate_rows, up_rows, down_far)
    )

    pair_rows = swap(own_rows, "yl")
    own_far = swap(own_rows, "c")
    pair_rows, own_far = lax.optimization_barrier((pair_rows, own_far))
    pair_far = swap(pair_rows, "c")
    cores = core.astype(jnp.int32).reshape(1)
    block_spec = pl.BlockSpec(block.shape, lambda i, c: (0, 0, 0))
    fixed = lambda i, c: (0, 0)
    on_chip = pl.pallas_call(
        functools.partial(down_kernel, capacity),
        out_shape=jax.ShapeDtypeStruct((slots_all, half), bf16),
        grid_spec=pltpu.PrefetchScalarGridSpec(
            num_scalar_prefetch=1,
            grid=(1,),
            in_specs=[block_spec] * 4
            + [
                pl.BlockSpec((feats, half), lambda i, c: (0, c[0])),
                pl.BlockSpec((feats, half), fixed),
                pl.BlockSpec(pick_rows.shape, fixed),
                pl.BlockSpec(rank_of.shape, fixed),
            ],
            out_specs=pl.BlockSpec((slots_all, half), fixed),
        ),
        compiler_params=BIG,
    )(cores, own_rows, own_far, pair_rows, pair_far, down, down_far, pick_rows, rank_of)
    pieces = over_x(on_chip.reshape(chips, slots_all // chips, half))
    near = over_x(
        whole(add_kernel, jax.ShapeDtypeStruct(pieces.shape, bf16), pieces)
    ).reshape(slots_all, half)
    far = swap(near, "c")

    def routes_of(side, near, far):
        rows_of = lambda i, c: (side, 0)
        hidden_of = lambda i, c: (side, c[0] ^ i)
        weights_of = lambda i, c: (0, c[0] ^ i)
        return pl.pallas_call(
            functools.partial(route_kernel, capacity),
            out_shape=block,
            grid_spec=pltpu.PrefetchScalarGridSpec(
                num_scalar_prefetch=1,
                grid=(2,),
                in_specs=[
                    pl.BlockSpec((slots_side, half), rows_of),
                    pl.BlockSpec((slots_side, half), rows_of),
                    pl.BlockSpec((slots_side, half), hidden_of),
                    pl.BlockSpec((slots_side, half), hidden_of),
                    pl.BlockSpec((feats, half), weights_of),
                    pl.BlockSpec((feats, half), weights_of),
                    pl.BlockSpec(put_all.shape, fixed),
                    pl.BlockSpec(rank_of.shape, fixed),
                ],
                out_specs=block_spec,
                scratch_shapes=[
                    pltpu.VMEM((slots_side, feats), jnp.float32),
                    pltpu.VMEM((slots_side, 1), jnp.float32),
                ],
            ),
            compiler_params=BIG,
        )(cores, near, far, gate_rows, up_rows, w_gate[0], w_up[0], put_all, rank_of)

    pair_routes = routes_of(1, near, far)
    pair_back = swap(pair_routes, "yl")
    far, _ = lax.optimization_barrier((far, pair_routes))
    own_routes = routes_of(0, near, far)
    both = whole(sum_kernel, block, own_routes, pair_back)
    returned = over_group(both)
    grad_in, grad_prob = whole(
        functools.partial(combine_kernel, capacity),
        (
            jax.ShapeDtypeStruct((feats, tokens), bf16),
            jax.ShapeDtypeStruct((2, tokens), bf16),
        ),
        returned,
        routes,
        gate_prob.T,
        widen,
        expert_of,
        rank_of,
        pick_all,
    )
    return (grad_in.T, grad_prob.T)


def solution(mesh):
    nodes, local = mesh.devices.shape
    rows = 8
    fine = Mesh(mesh.devices.reshape(nodes // rows, rows // 2, 2, local // 2, 2), (*NODE, "x", "c"))
    node, feats = NODE, ("x", "c")
    return jax.shard_map(
        shards,
        mesh=fine,
        in_specs=(
            P(node, feats),
            P(node, None),
            P(node, None),
            P(node, None, None),
            P(node, None, None),
            P(node, feats, None),
            P(node, feats, None),
            P(node, None, feats),
        ),
        out_specs=(P(node, feats), P(node, None)),
        check_vma=False,
    )
```

```python
import functools

import jax
import jax.numpy as jnp
import numpy as np
from jax import lax
from jax.experimental import pallas as pl
from jax.experimental.pallas import tpu as pltpu
from jax.sharding import Mesh
from jax.sharding import PartitionSpec as P

PAIR = ("z", "yh")
NODE = ("z", "yh", "yl")
LANES = 128
PACKED = 40
BATCH = 8


def swap(value, axis):
    return lax.ppermute(value, axis, ((0, 1), (1, 0)))


def times_transposed(left, right):
    return lax.dot_general(
        left, right, (((1,), (1,)), ((), ())), preferred_element_type=jnp.float32
    )


def over_x(blocks):
    return lax.all_to_all(blocks, "x", split_axis=0, concat_axis=0, tiled=True)


def turned(pair):
    return (pair % lax.axis_size("yh")) // (lax.axis_size("yh") // 2)


def over_group(blocks):
    pairs = lax.axis_size(PAIR)
    groups = [[2 * p + (g ^ turned(p)) for p in range(pairs)] for g in range(2)]
    return lax.all_to_all(
        blocks, NODE, split_axis=0, concat_axis=0, tiled=True, axis_index_groups=groups
    )


def packing(capacity):
    kinds = np.zeros((5, BATCH, capacity, BATCH, PACKED), np.float32)
    for block in range(BATCH):
        for slot in range(capacity):
            for kind in range(3):
                kinds[kind, block, slot, block, capacity * kind + slot] = 1
            kinds[3, block, slot, block, 3 * capacity + slot % (capacity // 2)] = 1
            kinds[4, block, slot, block, 3 * capacity + capacity // 2] = 1
    return kinds.reshape(5, BATCH * capacity, BATCH * PACKED)


def tail_lanes(rank, capacity):
    lane = lax.broadcasted_iota(jnp.int32, (rank.shape[0], LANES), 1)
    return (lane < LANES // 2) == (rank < capacity // 2)


def unpacked(block_ref, pick_ref, rank, capacity):
    span = BATCH * capacity
    features, probs = [], []
    for batch in range(block_ref.shape[0] // BATCH):
        rows = block_ref[batch * BATCH : (batch + 1) * BATCH].astype(jnp.float32)
        rows = rows.reshape(BATCH * PACKED, LANES).astype(jnp.bfloat16)
        picked = jnp.dot(pick_ref[...], rows, preferred_element_type=jnp.float32)
        own = rank[batch * span : (batch + 1) * span]
        tail = jnp.where(tail_lanes(own, capacity), picked[3 * span : 4 * span], 0.0)
        groups = [picked[k * span : (k + 1) * span] for k in range(3)] + [tail]
        features.append(jnp.concatenate(groups, axis=1).astype(jnp.bfloat16))
        if picked.shape[0] > 4 * span:
            lane = lax.broadcasted_iota(jnp.int32, (span, LANES), 1)
            prob = jnp.where(lane == own, picked[4 * span :], 0.0)
            probs.append(jnp.sum(prob, axis=1, keepdims=True))
    return features, probs


def pack(rows, probs, put_ref, rank, out_ref, capacity):
    span = BATCH * capacity
    for batch in range(out_ref.shape[0] // BATCH):
        own = rank[batch * span : (batch + 1) * span]
        part = rows[batch * span : (batch + 1) * span]
        tail = part[:, 3 * LANES :]
        tail = jnp.where(
            tail_lanes(own, capacity), jnp.concatenate([tail, tail], axis=1), 0.0
        )
        groups = [part[:, k * LANES : (k + 1) * LANES] for k in range(3)] + [tail]
        if probs is not None:
            lane = lax.broadcasted_iota(jnp.int32, (span, LANES), 1)
            groups.append(jnp.where(lane == own, probs[batch * span : (batch + 1) * span], 0.0))
        stacked = jnp.concatenate(groups, axis=0).astype(jnp.bfloat16)
        packed = jnp.dot(
            put_ref[:, : stacked.shape[0]], stacked, preferred_element_type=jnp.float32
        )
        out_ref[batch * BATCH : (batch + 1) * BATCH] = packed.reshape(
            BATCH, PACKED, LANES
        ).astype(jnp.bfloat16)


def slot_masks(routes, widen, expert, rank):
    experts = widen.shape[1]
    tokens = routes.shape[1]
    label = lax.broadcasted_iota(jnp.int32, (experts, tokens), 0)
    named = (routes[0:1] == label) | (routes[1:2] == label)
    earlier = lax.broadcasted_iota(jnp.int32, (tokens, tokens), 0) < lax.broadcasted_iota(
        jnp.int32, (tokens, tokens), 1
    )
    ones = jnp.where(named, 1.0, 0.0).astype(jnp.bfloat16)
    before = jnp.dot(
        ones, jnp.where(earlier, 1.0, 0.0).astype(jnp.bfloat16), preferred_element_type=jnp.float32
    )
    before = jnp.dot(widen, before.astype(jnp.bfloat16), preferred_element_type=jnp.float32)
    here = before == rank.astype(jnp.float32)
    return [here & (routes[k : k + 1] == expert) for k in range(2)]


def dispatch_kernel(capacity, routes_ref, grad_ref, widen_ref, expert_ref, rank_ref, put_ref, out_ref):
    first, second = slot_masks(routes_ref[...], widen_ref[...], expert_ref[...], rank_ref[...])
    mask = jnp.where(first | second, 1.0, 0.0).astype(jnp.bfloat16)
    rows = times_transposed(mask, grad_ref[...])
    pack(rows, None, put_ref, rank_ref[...], out_ref, capacity)


def stretched(weights):
    return jnp.concatenate([weights, weights[3 * LANES :]], axis=0)


def down_kernel(
    capacity, core_ref, block_ref, kept_w_ref, sent_w_ref, pick_ref, rank_ref, *refs
):
    kept_ref, sent_ref = refs[-2:]
    rows, _ = unpacked(block_ref, pick_ref, rank_ref[...], capacity)
    rows = jnp.concatenate(rows, axis=0)
    for weights_ref, out_ref in ((sent_w_ref, sent_ref), (kept_w_ref, kept_ref)):
        out_ref[...] = jnp.dot(
            rows, stretched(weights_ref[...]), preferred_element_type=jnp.float32
        ).astype(jnp.bfloat16)


def add_kernel(pieces_ref, out_ref):
    total = pieces_ref[0].astype(jnp.float32)
    for piece in range(1, pieces_ref.shape[0]):
        total = total + pieces_ref[piece].astype(jnp.float32)
    total = total.astype(jnp.bfloat16)
    for piece in range(out_ref.shape[0]):
        out_ref[piece] = total


def route_kernel(
    capacity,
    core_ref,
    near_ref,
    far_ref,
    gate_ref,
    up_ref,
    w_gate_ref,
    w_up_ref,
    put_ref,
    rank_ref,
    out_ref,
    total_ref,
    prob_ref,
):
    step = pl.program_id(0)

    @pl.when(step == 0)
    def _():
        total_ref[...] = jnp.zeros_like(total_ref)
        prob_ref[...] = jnp.zeros_like(prob_ref)

    units = jnp.where(step == 0, near_ref[...].astype(jnp.float32), far_ref[...].astype(jnp.float32))
    gate = gate_ref[...].astype(jnp.float32)
    up = up_ref[...].astype(jnp.float32)
    sigmoid = 1.0 / (1.0 + jnp.exp(-gate))
    upper = units * (gate * sigmoid)
    gates = units * up * sigmoid * (1.0 + gate * (1.0 - sigmoid))
    prob_ref[...] += jnp.sum(upper * up, axis=1, keepdims=True)
    total_ref[...] += times_transposed(
        gates.astype(jnp.bfloat16), w_gate_ref[...]
    ) + times_transposed(upper.astype(jnp.bfloat16), w_up_ref[...])

    @pl.when(step == 1)
    def _():
        pack(total_ref[...], prob_ref[...], put_ref, rank_ref[...], out_ref, capacity)


def sum_kernel(left_ref, right_ref, out_ref):
    out_ref[...] = (
        left_ref[...].astype(jnp.float32) + right_ref[...].astype(jnp.float32)
    ).astype(jnp.bfloat16)


def combine_kernel(
    capacity,
    back_ref,
    routes_ref,
    weight_ref,
    widen_ref,
    expert_ref,
    rank_ref,
    pick_ref,
    out_ref,
    prob_ref,
):
    masks = slot_masks(routes_ref[...], widen_ref[...], expert_ref[...], rank_ref[...])
    weights = jnp.where(masks[0], weight_ref[0:1], 0.0) + jnp.where(masks[1], weight_ref[1:2], 0.0)
    features, probs = unpacked(back_ref, pick_ref, rank_ref[...], capacity)
    wide = jnp.concatenate(features, axis=0)
    half = LANES // 2
    tail = wide[:, 3 * LANES : 3 * LANES + half] + wide[:, 3 * LANES + half :]
    rows = jnp.concatenate([wide[:, : 3 * LANES], tail], axis=1)
    total = jnp.zeros(out_ref.shape, jnp.float32)
    rest = weights
    for _ in range(3):
        part = rest.astype(jnp.bfloat16)
        rest = rest - part.astype(jnp.float32)
        total = total + lax.dot_general(
            rows, part, (((0,), (0,)), ((), ())), preferred_element_type=jnp.float32
        )
    out_ref[...] = total.astype(jnp.bfloat16)
    prob = jnp.concatenate(probs, axis=0)
    for k in range(2):
        prob_ref[k : k + 1] = jnp.sum(
            jnp.where(masks[k], prob, 0.0), axis=0, keepdims=True
        ).astype(jnp.bfloat16)


BIG = pltpu.CompilerParams(vmem_limit_bytes=40 * 1024 * 1024)
FULL = pltpu.CompilerParams(vmem_limit_bytes=60 * 1024 * 1024)


def cost(products, moved):
    return pl.CostEstimate(flops=2 * products, bytes_accessed=2 * moved, transcendentals=0)


def whole(kernel, out_shape, *args, params=BIG, estimate=None):
    return pl.pallas_call(
        kernel, out_shape=out_shape, compiler_params=params, cost_estimate=estimate
    )(*args)


def shards(grad_out, route_expert, gate_prob, saved_gate, saved_up, w_gate, w_up, w_down):
    experts = lax.axis_size(PAIR)
    chips = lax.axis_size("x")
    slots_all = saved_gate.shape[2]
    slots_side = slots_all // 2
    capacity = slots_side // experts
    feats = grad_out.shape[1]
    tokens = grad_out.shape[0]
    half = saved_gate.shape[1] // 2
    bf16 = jnp.bfloat16
    core = lax.axis_index("c")
    group = lax.axis_index("yl") ^ turned(lax.axis_index("yh"))
    numbers = np.arange(slots_side, dtype=np.int32)[:, None]
    expert_of = jnp.asarray(numbers // capacity)
    rank_of = jnp.asarray(numbers % capacity)
    widen = jnp.asarray(numbers // capacity == np.arange(experts)[None, :], bf16)
    kinds = packing(capacity)
    pick_all = jnp.asarray(kinds.reshape(-1, kinds.shape[2]), bf16)
    pick_rows = pick_all[: 4 * kinds.shape[1]]
    put_all = jnp.asarray(kinds.reshape(-1, kinds.shape[2]).T, bf16)
    block = jax.ShapeDtypeStruct((experts, PACKED, LANES), bf16)

    routes = route_expert.T
    outgoing = whole(
        functools.partial(dispatch_kernel, capacity),
        block,
        routes,
        grad_out.T,
        widen,
        expert_of,
        rank_of,
        put_all[:, : 4 * kinds.shape[1]],
        params=FULL,
    )
    own_rows = over_group(outgoing)

    slot = jnp.arange(slots_all, dtype=jnp.int32)[:, None]
    place = jnp.arange(slots_all, dtype=jnp.int32)[None, :]
    pair = slot // capacity % experts
    member = group ^ turned(pair) ^ (slot // slots_side)
    source = (2 * pair + member) * capacity + slot % capacity
    order = (place == source).astype(bf16)
    gate_rows = times_transposed(order, saved_gate[0]).astype(bf16)
    up_rows = times_transposed(order, saved_up[0]).astype(bf16)
    down = w_down[0].T
    own_rows, gate_rows, up_rows = lax.optimization_barrier((own_rows, gate_rows, up_rows))

    pair_rows = swap(own_rows, "yl")
    cores = core.astype(jnp.int32).reshape(1)
    block_spec = pl.BlockSpec(block.shape, lambda i, c: (0, 0, 0))
    fixed = lambda i, c: (0, 0)
    product = jax.ShapeDtypeStruct((slots_all, half), bf16)

    def products_of(side, rows, *filled):
        return pl.pallas_call(
            functools.partial(down_kernel, capacity),
            out_shape=(product, product),
            grid_spec=pltpu.PrefetchScalarGridSpec(
                num_scalar_prefetch=1,
                grid=(1,),
                in_specs=[
                    block_spec,
                    pl.BlockSpec((feats, half), lambda i, c: (0, c[0])),
                    pl.BlockSpec((feats, half), lambda i, c: (0, 1 - c[0])),
                    pl.BlockSpec(pick_rows.shape, fixed),
                    pl.BlockSpec(rank_of.shape, fixed),
                ]
                + [pl.BlockSpec(memory_space=pl.ANY)] * len(filled),
                out_specs=[pl.BlockSpec((slots_side, half), lambda i, c: (side, 0))] * 2,
            ),
            input_output_aliases={6 + i: i for i in range(len(filled))},
            compiler_params=BIG,
            cost_estimate=cost(
                2 * slots_side * feats * half, 2 * feats * half + 3 * slots_side * half
            ),
        )(cores, rows, down, down, pick_rows, rank_of, *filled)

    kept, sent = products_of(1, pair_rows, *products_of(0, own_rows))
    on_chip = whole(sum_kernel, product, kept, swap(sent, "c"))
    pieces = over_x(on_chip.reshape(chips, slots_all // chips, half))
    near = over_x(
        whole(add_kernel, jax.ShapeDtypeStruct(pieces.shape, bf16), pieces)
    ).reshape(slots_all, half)
    far = swap(near, "c")

    def routes_of(side, near, far):
        rows_of = lambda i, c: (side, 0)
        hidden_of = lambda i, c: (side, c[0] ^ i)
        weights_of = lambda i, c: (0, c[0] ^ i)
        return pl.pallas_call(
            functools.partial(route_kernel, capacity),
            out_shape=block,
            grid_spec=pltpu.PrefetchScalarGridSpec(
                num_scalar_prefetch=1,
                grid=(2,),
                in_specs=[
                    pl.BlockSpec((slots_side, half), rows_of),
                    pl.BlockSpec((slots_side, half), rows_of),
                    pl.BlockSpec((slots_side, half), hidden_of),
                    pl.BlockSpec((slots_side, half), hidden_of),
                    pl.BlockSpec((feats, half), weights_of),
                    pl.BlockSpec((feats, half), weights_of),
                    pl.BlockSpec(put_all.shape, fixed),
                    pl.BlockSpec(rank_of.shape, fixed),
                ],
                out_specs=block_spec,
                scratch_shapes=[
                    pltpu.VMEM((slots_side, feats), jnp.float32),
                    pltpu.VMEM((slots_side, 1), jnp.float32),
                ],
            ),
            compiler_params=BIG,
        )(cores, near, far, gate_rows, up_rows, w_gate[0], w_up[0], put_all, rank_of)

    pair_routes = routes_of(1, near, far)
    pair_back = swap(pair_routes, "yl")
    far, _ = lax.optimization_barrier((far, pair_routes))
    own_routes = routes_of(0, near, far)
    both = whole(sum_kernel, block, own_routes, pair_back)
    returned = over_group(both)
    grad_in, grad_prob = whole(
        functools.partial(combine_kernel, capacity),
        (
            jax.ShapeDtypeStruct((feats, tokens), bf16),
            jax.ShapeDtypeStruct((2, tokens), bf16),
        ),
        returned,
        routes,
        gate_prob.T,
        widen,
        expert_of,
        rank_of,
        pick_all,
    )
    return (grad_in.T, grad_prob.T)


def solution(mesh):
    nodes, local = mesh.devices.shape
    rows = 8
    fine = Mesh(mesh.devices.reshape(nodes // rows, rows // 2, 2, local // 2, 2), (*NODE, "x", "c"))
    node, feats = NODE, ("x", "c")
    return jax.shard_map(
        shards,
        mesh=fine,
        in_specs=(
            P(node, feats),
            P(node, None),
            P(node, None),
            P(node, None, None),
            P(node, None, None),
            P(node, feats, None),
            P(node, feats, None),
            P(node, None, feats),
        ),
        out_specs=(P(node, feats), P(node, None)),
        check_vma=False,
    )
```

```python
import functools

import jax
import jax.numpy as jnp
import numpy as np
from jax import lax
from jax.experimental import pallas as pl
from jax.experimental.pallas import tpu as pltpu
from jax.sharding import Mesh
from jax.sharding import PartitionSpec as P

PAIR = ("z", "yh")
NODE = ("z", "yh", "yl")
LANES = 128
PACKED = 40
BATCH = 8


def swap(value, axis):
    return lax.ppermute(value, axis, ((0, 1), (1, 0)))


def times_transposed(left, right):
    return lax.dot_general(
        left, right, (((1,), (1,)), ((), ())), preferred_element_type=jnp.float32
    )


def over_x(blocks):
    return lax.all_to_all(blocks, "x", split_axis=0, concat_axis=0, tiled=True)


def turned(pair):
    return (pair % lax.axis_size("yh")) // (lax.axis_size("yh") // 2)


def over_group(blocks):
    pairs = lax.axis_size(PAIR)
    groups = [[2 * p + (g ^ turned(p)) for p in range(pairs)] for g in range(2)]
    return lax.all_to_all(
        blocks, NODE, split_axis=0, concat_axis=0, tiled=True, axis_index_groups=groups
    )


def packing(capacity):
    kinds = np.zeros((5, BATCH, capacity, BATCH, PACKED), np.float32)
    for block in range(BATCH):
        for slot in range(capacity):
            for kind in range(3):
                kinds[kind, block, slot, block, capacity * kind + slot] = 1
            kinds[3, block, slot, block, 3 * capacity + slot % (capacity // 2)] = 1
            kinds[4, block, slot, block, 3 * capacity + capacity // 2] = 1
    return kinds.reshape(5, BATCH * capacity, BATCH * PACKED)


def tail_lanes(rank, capacity):
    lane = lax.broadcasted_iota(jnp.int32, (rank.shape[0], LANES), 1)
    return (lane < LANES // 2) == (rank < capacity // 2)


def unpacked(block_ref, pick_ref, rank, capacity):
    span = BATCH * capacity
    features, probs = [], []
    for batch in range(block_ref.shape[0] // BATCH):
        rows = block_ref[batch * BATCH : (batch + 1) * BATCH].astype(jnp.float32)
        rows = rows.reshape(BATCH * PACKED, LANES).astype(jnp.bfloat16)
        picked = jnp.dot(pick_ref[...], rows, preferred_element_type=jnp.float32)
        own = rank[batch * span : (batch + 1) * span]
        tail = jnp.where(tail_lanes(own, capacity), picked[3 * span : 4 * span], 0.0)
        groups = [picked[k * span : (k + 1) * span] for k in range(3)] + [tail]
        features.append(jnp.concatenate(groups, axis=1).astype(jnp.bfloat16))
        if picked.shape[0] > 4 * span:
            lane = lax.broadcasted_iota(jnp.int32, (span, LANES), 1)
            prob = jnp.where(lane == own, picked[4 * span :], 0.0)
            probs.append(jnp.sum(prob, axis=1, keepdims=True))
    return features, probs


def pack(rows, probs, put_ref, rank, out_ref, capacity):
    span = BATCH * capacity
    for batch in range(out_ref.shape[0] // BATCH):
        own = rank[batch * span : (batch + 1) * span]
        part = rows[batch * span : (batch + 1) * span]
        tail = part[:, 3 * LANES :]
        tail = jnp.where(
            tail_lanes(own, capacity), jnp.concatenate([tail, tail], axis=1), 0.0
        )
        groups = [part[:, k * LANES : (k + 1) * LANES] for k in range(3)] + [tail]
        if probs is not None:
            lane = lax.broadcasted_iota(jnp.int32, (span, LANES), 1)
            groups.append(jnp.where(lane == own, probs[batch * span : (batch + 1) * span], 0.0))
        stacked = jnp.concatenate(groups, axis=0).astype(jnp.bfloat16)
        packed = jnp.dot(
            put_ref[:, : stacked.shape[0]], stacked, preferred_element_type=jnp.float32
        )
        out_ref[batch * BATCH : (batch + 1) * BATCH] = packed.reshape(
            BATCH, PACKED, LANES
        ).astype(jnp.bfloat16)


def slot_masks(routes, widen, expert, rank):
    experts = widen.shape[1]
    tokens = routes.shape[1]
    label = lax.broadcasted_iota(jnp.int32, (experts, tokens), 0)
    named = (routes[0:1] == label) | (routes[1:2] == label)
    earlier = lax.broadcasted_iota(jnp.int32, (tokens, tokens), 0) < lax.broadcasted_iota(
        jnp.int32, (tokens, tokens), 1
    )
    ones = jnp.where(named, 1.0, 0.0).astype(jnp.bfloat16)
    before = jnp.dot(
        ones, jnp.where(earlier, 1.0, 0.0).astype(jnp.bfloat16), preferred_element_type=jnp.float32
    )
    before = jnp.dot(widen, before.astype(jnp.bfloat16), preferred_element_type=jnp.float32)
    here = before == rank.astype(jnp.float32)
    return [here & (routes[k : k + 1] == expert) for k in range(2)]


def dispatch_kernel(capacity, routes_ref, grad_ref, widen_ref, expert_ref, rank_ref, put_ref, out_ref):
    first, second = slot_masks(routes_ref[...], widen_ref[...], expert_ref[...], rank_ref[...])
    mask = jnp.where(first | second, 1.0, 0.0).astype(jnp.bfloat16)
    rows = times_transposed(mask, grad_ref[...])
    pack(rows, None, put_ref, rank_ref[...], out_ref, capacity)


def stretched(weights):
    return jnp.concatenate([weights, weights[3 * LANES :]], axis=0)


def down_kernel(
    capacity, core_ref, block_ref, kept_w_ref, sent_w_ref, pick_ref, rank_ref, *refs
):
    kept_ref, sent_ref = refs[-2:]
    rows, _ = unpacked(block_ref, pick_ref, rank_ref[...], capacity)
    rows = jnp.concatenate(rows, axis=0)
    for weights_ref, out_ref in ((sent_w_ref, sent_ref), (kept_w_ref, kept_ref)):
        total = jnp.dot(rows, stretched(weights_ref[...]), preferred_element_type=jnp.float32)
        out_ref[...] = total.reshape(out_ref.shape).astype(jnp.bfloat16)


def add_kernel(pieces_ref, own_ref, pair_ref):
    total = pieces_ref[0].astype(jnp.float32)
    for piece in range(1, pieces_ref.shape[0]):
        total = total + pieces_ref[piece].astype(jnp.float32)
    total = total.astype(jnp.bfloat16)
    for piece in range(pieces_ref.shape[0]):
        own_ref[piece] = total[0]
        pair_ref[piece] = total[1]


def route_kernel(
    capacity,
    core_ref,
    near_ref,
    far_ref,
    gate_ref,
    up_ref,
    w_gate_ref,
    w_up_ref,
    put_ref,
    rank_ref,
    out_ref,
    total_ref,
    prob_ref,
):
    step = pl.program_id(0)

    @pl.when(step == 0)
    def _():
        total_ref[...] = jnp.zeros_like(total_ref)
        prob_ref[...] = jnp.zeros_like(prob_ref)

    units = jnp.where(step == 0, near_ref[...].astype(jnp.float32), far_ref[...].astype(jnp.float32))
    gate = gate_ref[...].astype(jnp.float32)
    up = up_ref[...].astype(jnp.float32)
    sigmoid = 1.0 / (1.0 + jnp.exp(-gate))
    upper = units * (gate * sigmoid)
    gates = units * up * sigmoid * (1.0 + gate * (1.0 - sigmoid))
    prob_ref[...] += jnp.sum(upper * up, axis=1, keepdims=True)
    total_ref[...] += times_transposed(
        gates.astype(jnp.bfloat16), w_gate_ref[...]
    ) + times_transposed(upper.astype(jnp.bfloat16), w_up_ref[...])

    @pl.when(step == 1)
    def _():
        pack(total_ref[...], prob_ref[...], put_ref, rank_ref[...], out_ref, capacity)


def sum_kernel(left_ref, right_ref, out_ref):
    out_ref[...] = (
        left_ref[...].astype(jnp.float32) + right_ref[...].astype(jnp.float32)
    ).astype(jnp.bfloat16)


def combine_kernel(
    capacity,
    back_ref,
    routes_ref,
    weight_ref,
    widen_ref,
    expert_ref,
    rank_ref,
    pick_ref,
    out_ref,
    prob_ref,
):
    masks = slot_masks(routes_ref[...], widen_ref[...], expert_ref[...], rank_ref[...])
    weights = jnp.where(masks[0], weight_ref[0:1], 0.0) + jnp.where(masks[1], weight_ref[1:2], 0.0)
    features, probs = unpacked(back_ref, pick_ref, rank_ref[...], capacity)
    wide = jnp.concatenate(features, axis=0)
    half = LANES // 2
    tail = wide[:, 3 * LANES : 3 * LANES + half] + wide[:, 3 * LANES + half :]
    rows = jnp.concatenate([wide[:, : 3 * LANES], tail], axis=1)
    total = jnp.zeros(out_ref.shape, jnp.float32)
    rest = weights
    for _ in range(3):
        part = rest.astype(jnp.bfloat16)
        rest = rest - part.astype(jnp.float32)
        total = total + lax.dot_general(
            rows, part, (((0,), (0,)), ((), ())), preferred_element_type=jnp.float32
        )
    out_ref[...] = total.astype(jnp.bfloat16)
    prob = jnp.concatenate(probs, axis=0)
    for k in range(2):
        prob_ref[k : k + 1] = jnp.sum(
            jnp.where(masks[k], prob, 0.0), axis=0, keepdims=True
        ).astype(jnp.bfloat16)


BIG = pltpu.CompilerParams(vmem_limit_bytes=40 * 1024 * 1024)
FULL = pltpu.CompilerParams(vmem_limit_bytes=60 * 1024 * 1024)


def cost(products, moved):
    return pl.CostEstimate(flops=2 * products, bytes_accessed=2 * moved, transcendentals=0)


def whole(kernel, out_shape, *args, params=BIG, estimate=None):
    return pl.pallas_call(
        kernel, out_shape=out_shape, compiler_params=params, cost_estimate=estimate
    )(*args)


def shards(grad_out, route_expert, gate_prob, saved_gate, saved_up, w_gate, w_up, w_down):
    experts = lax.axis_size(PAIR)
    chips = lax.axis_size("x")
    slots_all = saved_gate.shape[2]
    slots_side = slots_all // 2
    capacity = slots_side // experts
    feats = grad_out.shape[1]
    tokens = grad_out.shape[0]
    half = saved_gate.shape[1] // 2
    bf16 = jnp.bfloat16
    core = lax.axis_index("c")
    group = lax.axis_index("yl") ^ turned(lax.axis_index("yh"))
    numbers = np.arange(slots_side, dtype=np.int32)[:, None]
    expert_of = jnp.asarray(numbers // capacity)
    rank_of = jnp.asarray(numbers % capacity)
    widen = jnp.asarray(numbers // capacity == np.arange(experts)[None, :], bf16)
    kinds = packing(capacity)
    pick_all = jnp.asarray(kinds.reshape(-1, kinds.shape[2]), bf16)
    pick_rows = pick_all[: 4 * kinds.shape[1]]
    put_all = jnp.asarray(kinds.reshape(-1, kinds.shape[2]).T, bf16)
    block = jax.ShapeDtypeStruct((experts, PACKED, LANES), bf16)

    routes = route_expert.T
    outgoing = whole(
        functools.partial(dispatch_kernel, capacity),
        block,
        routes,
        grad_out.T,
        widen,
        expert_of,
        rank_of,
        put_all[:, : 4 * kinds.shape[1]],
        params=FULL,
    )
    own_rows = over_group(outgoing)

    slot = jnp.arange(slots_all, dtype=jnp.int32)[:, None]
    place = jnp.arange(slots_all, dtype=jnp.int32)[None, :]
    pair = slot // capacity % experts
    member = group ^ turned(pair) ^ (slot // slots_side)
    source = (2 * pair + member) * capacity + slot % capacity
    order = (place == source).astype(bf16)
    gate_rows = times_transposed(order, saved_gate[0]).astype(bf16)
    up_rows = times_transposed(order, saved_up[0]).astype(bf16)
    down = w_down[0].T
    own_rows, gate_rows, up_rows = lax.optimization_barrier((own_rows, gate_rows, up_rows))

    pair_rows = swap(own_rows, "yl")
    cores = core.astype(jnp.int32).reshape(1)
    block_spec = pl.BlockSpec(block.shape, lambda i, c: (0, 0, 0))
    fixed = lambda i, c: (0, 0)
    share = slots_side // chips
    product = jax.ShapeDtypeStruct((chips, 2, share, half), bf16)

    def products_of(side, rows, *filled):
        return pl.pallas_call(
            functools.partial(down_kernel, capacity),
            out_shape=(product, product),
            grid_spec=pltpu.PrefetchScalarGridSpec(
                num_scalar_prefetch=1,
                grid=(1,),
                in_specs=[
                    block_spec,
                    pl.BlockSpec((feats, half), lambda i, c: (0, c[0])),
                    pl.BlockSpec((feats, half), lambda i, c: (0, 1 - c[0])),
                    pl.BlockSpec(pick_rows.shape, fixed),
                    pl.BlockSpec(rank_of.shape, fixed),
                ]
                + [pl.BlockSpec(memory_space=pl.ANY)] * len(filled),
                out_specs=[pl.BlockSpec((chips, 1, share, half), lambda i, c: (0, side, 0, 0))] * 2,
            ),
            input_output_aliases={6 + i: i for i in range(len(filled))},
            compiler_params=BIG,
            cost_estimate=cost(
                2 * slots_side * feats * half, 2 * feats * half + 3 * slots_side * half
            ),
        )(cores, rows, down, down, pick_rows, rank_of, *filled)

    kept, sent = products_of(1, pair_rows, *products_of(0, own_rows))
    on_chip = whole(sum_kernel, product, kept, swap(sent, "c"))
    own_piece, pair_piece = whole(
        add_kernel,
        (jax.ShapeDtypeStruct((chips, share, half), bf16),) * 2,
        over_x(on_chip),
    )
    pair_near = over_x(pair_piece)
    own_piece, pair_near = lax.optimization_barrier((own_piece, pair_near))
    own_near = over_x(own_piece)

    def routes_of(side, near):
        far = swap(near, "c")
        near, far = (value.reshape(slots_side, half) for value in (near, far))
        hidden_of = lambda i, c: (side, c[0] ^ i)
        weights_of = lambda i, c: (0, c[0] ^ i)
        return pl.pallas_call(
            functools.partial(route_kernel, capacity),
            out_shape=block,
            grid_spec=pltpu.PrefetchScalarGridSpec(
                num_scalar_prefetch=1,
                grid=(2,),
                in_specs=[
                    pl.BlockSpec((slots_side, half), fixed),
                    pl.BlockSpec((slots_side, half), fixed),
                    pl.BlockSpec((slots_side, half), hidden_of),
                    pl.BlockSpec((slots_side, half), hidden_of),
                    pl.BlockSpec((feats, half), weights_of),
                    pl.BlockSpec((feats, half), weights_of),
                    pl.BlockSpec(put_all.shape, fixed),
                    pl.BlockSpec(rank_of.shape, fixed),
                ],
                out_specs=block_spec,
                scratch_shapes=[
                    pltpu.VMEM((slots_side, feats), jnp.float32),
                    pltpu.VMEM((slots_side, 1), jnp.float32),
                ],
            ),
            compiler_params=BIG,
            cost_estimate=cost(
                4 * slots_side * feats * half, 4 * feats * half + 8 * slots_side * half
            ),
        )(cores, near, far, gate_rows, up_rows, w_gate[0], w_up[0], put_all, rank_of)

    pair_back = swap(routes_of(1, pair_near), "yl")
    own_near, pair_back = lax.optimization_barrier((own_near, pair_back))
    own_routes = routes_of(0, own_near)
    both = whole(sum_kernel, block, own_routes, pair_back)
    returned = over_group(both)
    grad_in, grad_prob = whole(
        functools.partial(combine_kernel, capacity),
        (
            jax.ShapeDtypeStruct((feats, tokens), bf16),
            jax.ShapeDtypeStruct((2, tokens), bf16),
        ),
        returned,
        routes,
        gate_prob.T,
        widen,
        expert_of,
        rank_of,
        pick_all,
    )
    return (grad_in.T, grad_prob.T)


def solution(mesh):
    nodes, local = mesh.devices.shape
    rows = 8
    fine = Mesh(mesh.devices.reshape(nodes // rows, rows // 2, 2, local // 2, 2), (*NODE, "x", "c"))
    node, feats = NODE, ("x", "c")
    return jax.shard_map(
        shards,
        mesh=fine,
        in_specs=(
            P(node, feats),
            P(node, None),
            P(node, None),
            P(node, None, None),
            P(node, None, None),
            P(node, feats, None),
            P(node, feats, None),
            P(node, None, feats),
        ),
        out_specs=(P(node, feats), P(node, None)),
        check_vma=False,
    )
```

```python
import functools

import jax
import jax.numpy as jnp
import numpy as np
from jax import lax
from jax.experimental import pallas as pl
from jax.experimental.pallas import tpu as pltpu
from jax.sharding import Mesh
from jax.sharding import PartitionSpec as P

PAIR = ("z", "yh")
NODE = ("z", "yh", "yl")
LANES = 128
PACKED = 40
BATCH = 8


def swap(value, axis):
    return lax.ppermute(value, axis, ((0, 1), (1, 0)))


def times_transposed(left, right):
    return lax.dot_general(
        left, right, (((1,), (1,)), ((), ())), preferred_element_type=jnp.float32
    )


def over_x(blocks):
    return lax.all_to_all(blocks, "x", split_axis=0, concat_axis=0, tiled=True)


def turned(pair):
    return (pair % lax.axis_size("yh")) // (lax.axis_size("yh") // 2)


def over_group(blocks):
    pairs = lax.axis_size(PAIR)
    groups = [[2 * p + (g ^ turned(p)) for p in range(pairs)] for g in range(2)]
    return lax.all_to_all(
        blocks, NODE, split_axis=0, concat_axis=0, tiled=True, axis_index_groups=groups
    )


def packing(capacity):
    kinds = np.zeros((5, BATCH, capacity, BATCH, PACKED), np.float32)
    for block in range(BATCH):
        for slot in range(capacity):
            for kind in range(3):
                kinds[kind, block, slot, block, capacity * kind + slot] = 1
            kinds[3, block, slot, block, 3 * capacity + slot % (capacity // 2)] = 1
            kinds[4, block, slot, block, 3 * capacity + capacity // 2] = 1
    return kinds.reshape(5, BATCH * capacity, BATCH * PACKED)


def tail_lanes(rank, capacity):
    lane = lax.broadcasted_iota(jnp.int32, (rank.shape[0], LANES), 1)
    return (lane < LANES // 2) == (rank < capacity // 2)


def unpacked(block_ref, pick_ref, rank, capacity, places=None):
    span = BATCH * capacity
    features, probs = [], []
    for batch in range((len(places) if places else block_ref.shape[0]) // BATCH):
        here = slice(batch * BATCH, (batch + 1) * BATCH)
        if places:
            rows = jnp.concatenate([block_ref[n].astype(jnp.float32) for n in places[here]], axis=0)
        else:
            rows = block_ref[here].astype(jnp.float32).reshape(BATCH * PACKED, LANES)
        rows = rows.astype(jnp.bfloat16)
        picked = jnp.dot(pick_ref[...], rows, preferred_element_type=jnp.float32)
        own = rank[batch * span : (batch + 1) * span]
        tail = jnp.where(tail_lanes(own, capacity), picked[3 * span : 4 * span], 0.0)
        groups = [picked[k * span : (k + 1) * span] for k in range(3)] + [tail]
        features.append(jnp.concatenate(groups, axis=1).astype(jnp.bfloat16))
        if picked.shape[0] > 4 * span:
            lane = lax.broadcasted_iota(jnp.int32, (span, LANES), 1)
            prob = jnp.where(lane == own, picked[4 * span :], 0.0)
            probs.append(jnp.sum(prob, axis=1, keepdims=True))
    return features, probs


def pack(rows, probs, put_ref, rank, out_ref, capacity):
    span = BATCH * capacity
    for batch in range(out_ref.shape[0] // BATCH):
        own = rank[batch * span : (batch + 1) * span]
        part = rows[batch * span : (batch + 1) * span]
        tail = part[:, 3 * LANES :]
        tail = jnp.where(
            tail_lanes(own, capacity), jnp.concatenate([tail, tail], axis=1), 0.0
        )
        groups = [part[:, k * LANES : (k + 1) * LANES] for k in range(3)] + [tail]
        if probs is not None:
            lane = lax.broadcasted_iota(jnp.int32, (span, LANES), 1)
            groups.append(jnp.where(lane == own, probs[batch * span : (batch + 1) * span], 0.0))
        stacked = jnp.concatenate(groups, axis=0).astype(jnp.bfloat16)
        packed = jnp.dot(
            put_ref[:, : stacked.shape[0]], stacked, preferred_element_type=jnp.float32
        )
        packed = packed.reshape(BATCH, PACKED, LANES).astype(jnp.bfloat16)
        here = slice(batch * BATCH, (batch + 1) * BATCH)
        if len(out_ref.shape) == 3:
            out_ref[here] = packed
        else:
            for node in range(out_ref.shape[1]):
                out_ref[here, node] = packed


def slot_masks(routes, widen, expert, rank):
    experts = widen.shape[1]
    tokens = routes.shape[1]
    label = lax.broadcasted_iota(jnp.int32, (experts, tokens), 0)
    named = (routes[0:1] == label) | (routes[1:2] == label)
    earlier = lax.broadcasted_iota(jnp.int32, (tokens, tokens), 0) < lax.broadcasted_iota(
        jnp.int32, (tokens, tokens), 1
    )
    ones = jnp.where(named, 1.0, 0.0).astype(jnp.bfloat16)
    before = jnp.dot(
        ones, jnp.where(earlier, 1.0, 0.0).astype(jnp.bfloat16), preferred_element_type=jnp.float32
    )
    before = jnp.dot(widen, before.astype(jnp.bfloat16), preferred_element_type=jnp.float32)
    here = before == rank.astype(jnp.float32)
    return [here & (routes[k : k + 1] == expert) for k in range(2)]


def dispatch_kernel(capacity, routes_ref, grad_ref, widen_ref, expert_ref, rank_ref, put_ref, out_ref):
    first, second = slot_masks(routes_ref[...], widen_ref[...], expert_ref[...], rank_ref[...])
    mask = jnp.where(first | second, 1.0, 0.0).astype(jnp.bfloat16)
    rows = times_transposed(mask, grad_ref[...])
    pack(rows, None, put_ref, rank_ref[...], out_ref, capacity)


def stretched(weights):
    return jnp.concatenate([weights, weights[3 * LANES :]], axis=0)


def down_kernel(
    capacity,
    turns,
    where_ref,
    block_ref,
    kept_w_ref,
    sent_w_ref,
    pick_ref,
    rank_ref,
    kept_ref,
    sent_ref,
):
    sides = []
    for side in range(2):
        places = [2 * p + (where_ref[1] ^ (turn ^ side)) for p, turn in enumerate(turns)]
        sides += unpacked(block_ref, pick_ref, rank_ref[...], capacity, places)[0]
    rows = jnp.concatenate(sides, axis=0)
    for weights_ref, out_ref in ((sent_w_ref, sent_ref), (kept_w_ref, kept_ref)):
        out_ref[...] = jnp.dot(
            rows, stretched(weights_ref[...]), preferred_element_type=jnp.float32
        ).astype(jnp.bfloat16)


def add_kernel(pieces_ref, out_ref):
    total = pieces_ref[0].astype(jnp.float32)
    for piece in range(1, pieces_ref.shape[0]):
        total = total + pieces_ref[piece].astype(jnp.float32)
    total = total.astype(jnp.bfloat16)
    for piece in range(out_ref.shape[0]):
        out_ref[piece] = total


def route_kernel(
    capacity,
    core_ref,
    near_ref,
    far_ref,
    gate_ref,
    up_ref,
    w_gate_ref,
    w_up_ref,
    put_ref,
    rank_ref,
    out_ref,
    total_ref,
    prob_ref,
):
    step = pl.program_id(0)

    @pl.when(step == 0)
    def _():
        total_ref[...] = jnp.zeros_like(total_ref)
        prob_ref[...] = jnp.zeros_like(prob_ref)

    units = jnp.where(step == 0, near_ref[...].astype(jnp.float32), far_ref[...].astype(jnp.float32))
    gate = gate_ref[...].astype(jnp.float32)
    up = up_ref[...].astype(jnp.float32)
    sigmoid = 1.0 / (1.0 + jnp.exp(-gate))
    upper = units * (gate * sigmoid)
    gates = units * up * sigmoid * (1.0 + gate * (1.0 - sigmoid))
    prob_ref[...] += jnp.sum(upper * up, axis=1, keepdims=True)
    total_ref[...] += times_transposed(
        gates.astype(jnp.bfloat16), w_gate_ref[...]
    ) + times_transposed(upper.astype(jnp.bfloat16), w_up_ref[...])

    @pl.when(step == 1)
    def _():
        pack(total_ref[...], prob_ref[...], put_ref, rank_ref[...], out_ref, capacity)


def sum_kernel(left_ref, right_ref, out_ref):
    out_ref[...] = (
        left_ref[...].astype(jnp.float32) + right_ref[...].astype(jnp.float32)
    ).astype(jnp.bfloat16)


def combine_kernel(
    capacity,
    back_ref,
    routes_ref,
    weight_ref,
    widen_ref,
    expert_ref,
    rank_ref,
    pick_ref,
    out_ref,
    prob_ref,
):
    masks = slot_masks(routes_ref[...], widen_ref[...], expert_ref[...], rank_ref[...])
    weights = jnp.where(masks[0], weight_ref[0:1], 0.0) + jnp.where(masks[1], weight_ref[1:2], 0.0)
    features, probs = unpacked(back_ref, pick_ref, rank_ref[...], capacity)
    wide = jnp.concatenate(features, axis=0)
    half = LANES // 2
    tail = wide[:, 3 * LANES : 3 * LANES + half] + wide[:, 3 * LANES + half :]
    rows = jnp.concatenate([wide[:, : 3 * LANES], tail], axis=1)
    total = jnp.zeros(out_ref.shape, jnp.float32)
    rest = weights
    for _ in range(3):
        part = rest.astype(jnp.bfloat16)
        rest = rest - part.astype(jnp.float32)
        total = total + lax.dot_general(
            rows, part, (((0,), (0,)), ((), ())), preferred_element_type=jnp.float32
        )
    out_ref[...] = total.astype(jnp.bfloat16)
    prob = jnp.concatenate(probs, axis=0)
    for k in range(2):
        prob_ref[k : k + 1] = jnp.sum(
            jnp.where(masks[k], prob, 0.0), axis=0, keepdims=True
        ).astype(jnp.bfloat16)


BIG = pltpu.CompilerParams(vmem_limit_bytes=40 * 1024 * 1024)
FULL = pltpu.CompilerParams(vmem_limit_bytes=60 * 1024 * 1024)


def cost(products, moved):
    return pl.CostEstimate(flops=2 * products, bytes_accessed=2 * moved, transcendentals=0)


def whole(kernel, out_shape, *args, params=BIG, estimate=None):
    return pl.pallas_call(
        kernel, out_shape=out_shape, compiler_params=params, cost_estimate=estimate
    )(*args)


def shards(grad_out, route_expert, gate_prob, saved_gate, saved_up, w_gate, w_up, w_down):
    experts = lax.axis_size(PAIR)
    chips = lax.axis_size("x")
    slots_all = saved_gate.shape[2]
    slots_side = slots_all // 2
    capacity = slots_side // experts
    feats = grad_out.shape[1]
    tokens = grad_out.shape[0]
    half = saved_gate.shape[1] // 2
    bf16 = jnp.bfloat16
    core = lax.axis_index("c")
    group = lax.axis_index("yl") ^ turned(lax.axis_index("yh"))
    numbers = np.arange(slots_side, dtype=np.int32)[:, None]
    expert_of = jnp.asarray(numbers // capacity)
    rank_of = jnp.asarray(numbers % capacity)
    widen = jnp.asarray(numbers // capacity == np.arange(experts)[None, :], bf16)
    kinds = packing(capacity)
    pick_all = jnp.asarray(kinds.reshape(-1, kinds.shape[2]), bf16)
    pick_rows = pick_all[: 4 * kinds.shape[1]]
    put_all = jnp.asarray(kinds.reshape(-1, kinds.shape[2]).T, bf16)
    block = jax.ShapeDtypeStruct((experts, PACKED, LANES), bf16)

    routes = route_expert.T
    outgoing = whole(
        functools.partial(dispatch_kernel, capacity),
        jax.ShapeDtypeStruct((experts, 2, PACKED, LANES), bf16),
        routes,
        grad_out.T,
        widen,
        expert_of,
        rank_of,
        put_all[:, : 4 * kinds.shape[1]],
        params=FULL,
    )
    arrived = lax.all_to_all(
        outgoing.reshape(2 * experts, PACKED, LANES), NODE, split_axis=0, concat_axis=0, tiled=True
    )

    slot = jnp.arange(slots_all, dtype=jnp.int32)[:, None]
    place = jnp.arange(slots_all, dtype=jnp.int32)[None, :]
    pair = slot // capacity % experts
    member = group ^ turned(pair) ^ (slot // slots_side)
    source = (2 * pair + member) * capacity + slot % capacity
    order = (place == source).astype(bf16)
    gate_rows = times_transposed(order, saved_gate[0]).astype(bf16)
    up_rows = times_transposed(order, saved_up[0]).astype(bf16)
    down = w_down[0].T
    arrived, gate_rows, up_rows = lax.optimization_barrier((arrived, gate_rows, up_rows))

    cores = core.astype(jnp.int32).reshape(1)
    block_spec = pl.BlockSpec(block.shape, lambda i, c: (0, 0, 0))
    fixed = lambda i, c: (0, 0)
    product = jax.ShapeDtypeStruct((slots_all, half), bf16)
    kept, sent = pl.pallas_call(
        functools.partial(down_kernel, capacity, tuple(turned(p) for p in range(experts))),
        out_shape=(product, product),
        grid_spec=pltpu.PrefetchScalarGridSpec(
            num_scalar_prefetch=1,
            grid=(1,),
            in_specs=[
                pl.BlockSpec(arrived.shape, lambda i, c: (0, 0, 0)),
                pl.BlockSpec((feats, half), lambda i, c: (0, c[0])),
                pl.BlockSpec((feats, half), lambda i, c: (0, 1 - c[0])),
                pl.BlockSpec(pick_rows.shape, fixed),
                pl.BlockSpec(rank_of.shape, fixed),
            ],
            out_specs=[pl.BlockSpec((slots_all, half), fixed)] * 2,
        ),
        compiler_params=BIG,
    )(
        jnp.stack([core, group]).astype(jnp.int32),
        arrived,
        down,
        down,
        pick_rows,
        rank_of,
    )
    on_chip = whole(sum_kernel, product, kept, swap(sent, "c"))
    pieces = over_x(on_chip.reshape(chips, slots_all // chips, half))
    near = over_x(
        whole(add_kernel, jax.ShapeDtypeStruct(pieces.shape, bf16), pieces)
    ).reshape(slots_all, half)
    far = swap(near, "c")

    def routes_of(side, near, far):
        rows_of = lambda i, c: (side, 0)
        hidden_of = lambda i, c: (side, c[0] ^ i)
        weights_of = lambda i, c: (0, c[0] ^ i)
        return pl.pallas_call(
            functools.partial(route_kernel, capacity),
            out_shape=block,
            grid_spec=pltpu.PrefetchScalarGridSpec(
                num_scalar_prefetch=1,
                grid=(2,),
                in_specs=[
                    pl.BlockSpec((slots_side, half), rows_of),
                    pl.BlockSpec((slots_side, half), rows_of),
                    pl.BlockSpec((slots_side, half), hidden_of),
                    pl.BlockSpec((slots_side, half), hidden_of),
                    pl.BlockSpec((feats, half), weights_of),
                    pl.BlockSpec((feats, half), weights_of),
                    pl.BlockSpec(put_all.shape, fixed),
                    pl.BlockSpec(rank_of.shape, fixed),
                ],
                out_specs=block_spec,
                scratch_shapes=[
                    pltpu.VMEM((slots_side, feats), jnp.float32),
                    pltpu.VMEM((slots_side, 1), jnp.float32),
                ],
            ),
            compiler_params=BIG,
        )(cores, near, far, gate_rows, up_rows, w_gate[0], w_up[0], put_all, rank_of)

    pair_routes = routes_of(1, near, far)
    pair_back = swap(pair_routes, "yl")
    far, _ = lax.optimization_barrier((far, pair_routes))
    own_routes = routes_of(0, near, far)
    both = whole(sum_kernel, block, own_routes, pair_back)
    returned = over_group(both)
    grad_in, grad_prob = whole(
        functools.partial(combine_kernel, capacity),
        (
            jax.ShapeDtypeStruct((feats, tokens), bf16),
            jax.ShapeDtypeStruct((2, tokens), bf16),
        ),
        returned,
        routes,
        gate_prob.T,
        widen,
        expert_of,
        rank_of,
        pick_all,
    )
    return (grad_in.T, grad_prob.T)


def solution(mesh):
    nodes, local = mesh.devices.shape
    rows = 8
    fine = Mesh(mesh.devices.reshape(nodes // rows, rows // 2, 2, local // 2, 2), (*NODE, "x", "c"))
    node, feats = NODE, ("x", "c")
    return jax.shard_map(
        shards,
        mesh=fine,
        in_specs=(
            P(node, feats),
            P(node, None),
            P(node, None),
            P(node, None, None),
            P(node, None, None),
            P(node, feats, None),
            P(node, feats, None),
            P(node, None, feats),
        ),
        out_specs=(P(node, feats), P(node, None)),
        check_vma=False,
    )
```

```python
import functools

import jax
import jax.numpy as jnp
import numpy as np
from jax import lax
from jax.experimental import pallas as pl
from jax.experimental.pallas import tpu as pltpu
from jax.sharding import Mesh
from jax.sharding import PartitionSpec as P

PAIR = ("z", "yh")
NODE = ("z", "yh", "yl")
LANES = 128
PACKED = 40
BATCH = 8


def swap(value, axis):
    return lax.ppermute(value, axis, ((0, 1), (1, 0)))


def times_transposed(left, right):
    return lax.dot_general(
        left, right, (((1,), (1,)), ((), ())), preferred_element_type=jnp.float32
    )


def over_x(blocks):
    return lax.all_to_all(blocks, "x", split_axis=0, concat_axis=0, tiled=True)


def turned(pair):
    return (pair % lax.axis_size("yh")) // (lax.axis_size("yh") // 2)


def over_group(blocks):
    pairs = lax.axis_size(PAIR)
    groups = [[2 * p + (g ^ turned(p)) for p in range(pairs)] for g in range(2)]
    return lax.all_to_all(
        blocks, NODE, split_axis=0, concat_axis=0, tiled=True, axis_index_groups=groups
    )


def packing(capacity):
    kinds = np.zeros((5, BATCH, capacity, BATCH, PACKED), np.float32)
    for block in range(BATCH):
        for slot in range(capacity):
            for kind in range(3):
                kinds[kind, block, slot, block, capacity * kind + slot] = 1
            kinds[3, block, slot, block, 3 * capacity + slot % (capacity // 2)] = 1
            kinds[4, block, slot, block, 3 * capacity + capacity // 2] = 1
    return kinds.reshape(5, BATCH * capacity, BATCH * PACKED)


def tail_lanes(rank, capacity):
    lane = lax.broadcasted_iota(jnp.int32, (rank.shape[0], LANES), 1)
    return (lane < LANES // 2) == (rank < capacity // 2)


def unpacked(block_ref, pick_ref, rank, capacity, places=None):
    span = BATCH * capacity
    features, probs = [], []
    for batch in range((len(places) if places else block_ref.shape[0]) // BATCH):
        here = slice(batch * BATCH, (batch + 1) * BATCH)
        if places:
            rows = jnp.concatenate([block_ref[n].astype(jnp.float32) for n in places[here]], axis=0)
        else:
            rows = block_ref[here].astype(jnp.float32).reshape(BATCH * PACKED, LANES)
        rows = rows.astype(jnp.bfloat16)
        picked = jnp.dot(pick_ref[...], rows, preferred_element_type=jnp.float32)
        own = rank[batch * span : (batch + 1) * span]
        tail = jnp.where(tail_lanes(own, capacity), picked[3 * span : 4 * span], 0.0)
        groups = [picked[k * span : (k + 1) * span] for k in range(3)] + [tail]
        features.append(jnp.concatenate(groups, axis=1).astype(jnp.bfloat16))
        if picked.shape[0] > 4 * span:
            lane = lax.broadcasted_iota(jnp.int32, (span, LANES), 1)
            prob = jnp.where(lane == own, picked[4 * span :], 0.0)
            probs.append(jnp.sum(prob, axis=1, keepdims=True))
    return features, probs


def pack(rows, probs, put_ref, rank, out_ref, capacity):
    span = BATCH * capacity
    for batch in range(out_ref.shape[0] // BATCH):
        own = rank[batch * span : (batch + 1) * span]
        part = rows[batch * span : (batch + 1) * span]
        tail = part[:, 3 * LANES :]
        tail = jnp.where(
            tail_lanes(own, capacity), jnp.concatenate([tail, tail], axis=1), 0.0
        )
        groups = [part[:, k * LANES : (k + 1) * LANES] for k in range(3)] + [tail]
        if probs is not None:
            lane = lax.broadcasted_iota(jnp.int32, (span, LANES), 1)
            groups.append(jnp.where(lane == own, probs[batch * span : (batch + 1) * span], 0.0))
        stacked = jnp.concatenate(groups, axis=0).astype(jnp.bfloat16)
        packed = jnp.dot(
            put_ref[:, : stacked.shape[0]], stacked, preferred_element_type=jnp.float32
        )
        packed = packed.reshape(BATCH, PACKED, LANES).astype(jnp.bfloat16)
        here = slice(batch * BATCH, (batch + 1) * BATCH)
        if len(out_ref.shape) == 3:
            out_ref[here] = packed
        else:
            for node in range(out_ref.shape[1]):
                out_ref[here, node] = packed


def slot_masks(routes, widen, expert, rank):
    experts = widen.shape[1]
    tokens = routes.shape[1]
    label = lax.broadcasted_iota(jnp.int32, (experts, tokens), 0)
    named = (routes[0:1] == label) | (routes[1:2] == label)
    earlier = lax.broadcasted_iota(jnp.int32, (tokens, tokens), 0) < lax.broadcasted_iota(
        jnp.int32, (tokens, tokens), 1
    )
    ones = jnp.where(named, 1.0, 0.0).astype(jnp.bfloat16)
    before = jnp.dot(
        ones, jnp.where(earlier, 1.0, 0.0).astype(jnp.bfloat16), preferred_element_type=jnp.float32
    )
    before = jnp.dot(widen, before.astype(jnp.bfloat16), preferred_element_type=jnp.float32)
    here = before == rank.astype(jnp.float32)
    return [here & (routes[k : k + 1] == expert) for k in range(2)]


def dispatch_kernel(capacity, routes_ref, grad_ref, widen_ref, expert_ref, rank_ref, put_ref, out_ref):
    first, second = slot_masks(routes_ref[...], widen_ref[...], expert_ref[...], rank_ref[...])
    mask = jnp.where(first | second, 1.0, 0.0).astype(jnp.bfloat16)
    rows = times_transposed(mask, grad_ref[...])
    pack(rows, None, put_ref, rank_ref[...], out_ref, capacity)


def stretched(weights):
    return jnp.concatenate([weights, weights[3 * LANES :]], axis=0)


def down_kernel(
    capacity,
    turns,
    where_ref,
    block_ref,
    kept_w_ref,
    sent_w_ref,
    rank_ref,
    kept_ref,
    sent_ref,
    pick_ref,
):
    span = BATCH * capacity
    rank = rank_ref[: 4 * span]
    row = lax.broadcasted_iota(jnp.int32, rank.shape, 0)
    kind = sum((row >= span * k).astype(jnp.int32) for k in range(1, 4))
    fold = jnp.where((kind == 3) & (rank >= capacity // 2), capacity // 2, 0)
    target = (row - span * kind - rank) * (PACKED // capacity) + capacity * kind + rank - fold
    lane = lax.broadcasted_iota(jnp.int32, pick_ref.shape, 1)
    pick_ref[...] = jnp.where(lane == target, 1.0, 0.0).astype(jnp.bfloat16)
    sides = []
    for side in range(2):
        places = [2 * p + (where_ref[1] ^ (turn ^ side)) for p, turn in enumerate(turns)]
        sides += unpacked(block_ref, pick_ref, rank_ref[...], capacity, places)[0]
    rows = jnp.concatenate(sides, axis=0)
    for weights_ref, out_ref in ((sent_w_ref, sent_ref), (kept_w_ref, kept_ref)):
        out_ref[...] = jnp.dot(
            rows, stretched(weights_ref[...]), preferred_element_type=jnp.float32
        ).astype(jnp.bfloat16)


def add_kernel(pieces_ref, out_ref):
    total = pieces_ref[0].astype(jnp.float32)
    for piece in range(1, pieces_ref.shape[0]):
        total = total + pieces_ref[piece].astype(jnp.float32)
    total = total.astype(jnp.bfloat16)
    for piece in range(out_ref.shape[0]):
        out_ref[piece] = total


def route_kernel(
    capacity,
    core_ref,
    near_ref,
    far_ref,
    gate_ref,
    up_ref,
    w_gate_ref,
    w_up_ref,
    put_ref,
    rank_ref,
    out_ref,
    total_ref,
    prob_ref,
):
    step = pl.program_id(0)

    @pl.when(step == 0)
    def _():
        total_ref[...] = jnp.zeros_like(total_ref)
        prob_ref[...] = jnp.zeros_like(prob_ref)

    units = jnp.where(step == 0, near_ref[...].astype(jnp.float32), far_ref[...].astype(jnp.float32))
    gate = gate_ref[...].astype(jnp.float32)
    up = up_ref[...].astype(jnp.float32)
    sigmoid = 1.0 / (1.0 + jnp.exp(-gate))
    upper = units * (gate * sigmoid)
    gates = units * up * sigmoid * (1.0 + gate * (1.0 - sigmoid))
    prob_ref[...] += jnp.sum(upper * up, axis=1, keepdims=True)
    total_ref[...] += times_transposed(
        gates.astype(jnp.bfloat16), w_gate_ref[...]
    ) + times_transposed(upper.astype(jnp.bfloat16), w_up_ref[...])

    @pl.when(step == 1)
    def _():
        pack(total_ref[...], prob_ref[...], put_ref, rank_ref[...], out_ref, capacity)


def sum_kernel(left_ref, right_ref, out_ref):
    out_ref[...] = (
        left_ref[...].astype(jnp.float32) + right_ref[...].astype(jnp.float32)
    ).astype(jnp.bfloat16)


def combine_kernel(
    capacity,
    back_ref,
    routes_ref,
    weight_ref,
    widen_ref,
    expert_ref,
    rank_ref,
    pick_ref,
    out_ref,
    prob_ref,
):
    masks = slot_masks(routes_ref[...], widen_ref[...], expert_ref[...], rank_ref[...])
    weights = jnp.where(masks[0], weight_ref[0:1], 0.0) + jnp.where(masks[1], weight_ref[1:2], 0.0)
    features, probs = unpacked(back_ref, pick_ref, rank_ref[...], capacity)
    wide = jnp.concatenate(features, axis=0)
    half = LANES // 2
    tail = wide[:, 3 * LANES : 3 * LANES + half] + wide[:, 3 * LANES + half :]
    rows = jnp.concatenate([wide[:, : 3 * LANES], tail], axis=1)
    total = jnp.zeros(out_ref.shape, jnp.float32)
    rest = weights
    for _ in range(3):
        part = rest.astype(jnp.bfloat16)
        rest = rest - part.astype(jnp.float32)
        total = total + lax.dot_general(
            rows, part, (((0,), (0,)), ((), ())), preferred_element_type=jnp.float32
        )
    out_ref[...] = total.astype(jnp.bfloat16)
    prob = jnp.concatenate(probs, axis=0)
    for k in range(2):
        prob_ref[k : k + 1] = jnp.sum(
            jnp.where(masks[k], prob, 0.0), axis=0, keepdims=True
        ).astype(jnp.bfloat16)


BIG = pltpu.CompilerParams(vmem_limit_bytes=40 * 1024 * 1024)
FULL = pltpu.CompilerParams(vmem_limit_bytes=60 * 1024 * 1024)


def cost(products, moved):
    return pl.CostEstimate(flops=2 * products, bytes_accessed=2 * moved, transcendentals=0)


def whole(kernel, out_shape, *args, params=BIG, estimate=None):
    return pl.pallas_call(
        kernel, out_shape=out_shape, compiler_params=params, cost_estimate=estimate
    )(*args)


def shards(grad_out, route_expert, gate_prob, saved_gate, saved_up, w_gate, w_up, w_down):
    experts = lax.axis_size(PAIR)
    chips = lax.axis_size("x")
    slots_all = saved_gate.shape[2]
    slots_side = slots_all // 2
    capacity = slots_side // experts
    feats = grad_out.shape[1]
    tokens = grad_out.shape[0]
    half = saved_gate.shape[1] // 2
    bf16 = jnp.bfloat16
    core = lax.axis_index("c")
    group = lax.axis_index("yl") ^ turned(lax.axis_index("yh"))
    numbers = np.arange(slots_side, dtype=np.int32)[:, None]
    expert_of = jnp.asarray(numbers // capacity)
    rank_of = jnp.asarray(numbers % capacity)
    widen = jnp.asarray(numbers // capacity == np.arange(experts)[None, :], bf16)
    kinds = packing(capacity)
    pick_all = jnp.asarray(kinds.reshape(-1, kinds.shape[2]), bf16)
    put_all = jnp.asarray(kinds.reshape(-1, kinds.shape[2]).T, bf16)
    block = jax.ShapeDtypeStruct((experts, PACKED, LANES), bf16)

    routes = route_expert.T
    outgoing = whole(
        functools.partial(dispatch_kernel, capacity),
        jax.ShapeDtypeStruct((experts, 2, PACKED, LANES), bf16),
        routes,
        grad_out.T,
        widen,
        expert_of,
        rank_of,
        put_all[:, : 4 * kinds.shape[1]],
        params=FULL,
    )
    arrived = lax.all_to_all(
        outgoing.reshape(2 * experts, PACKED, LANES), NODE, split_axis=0, concat_axis=0, tiled=True
    )

    slot = jnp.arange(slots_all, dtype=jnp.int32)[:, None]
    place = jnp.arange(slots_all, dtype=jnp.int32)[None, :]
    pair = slot // capacity % experts
    member = group ^ turned(pair) ^ (slot // slots_side)
    source = (2 * pair + member) * capacity + slot % capacity
    order = (place == source).astype(bf16)
    gate_rows = times_transposed(order, saved_gate[0]).astype(bf16)
    up_rows = times_transposed(order, saved_up[0]).astype(bf16)
    down = w_down[0].T
    arrived, gate_rows, up_rows = lax.optimization_barrier((arrived, gate_rows, up_rows))

    cores = core.astype(jnp.int32).reshape(1)
    block_spec = pl.BlockSpec(block.shape, lambda i, c: (0, 0, 0))
    fixed = lambda i, c: (0, 0)
    product = jax.ShapeDtypeStruct((slots_all, half), bf16)
    kept, sent = pl.pallas_call(
        functools.partial(down_kernel, capacity, tuple(turned(p) for p in range(experts))),
        out_shape=(product, product),
        grid_spec=pltpu.PrefetchScalarGridSpec(
            num_scalar_prefetch=1,
            grid=(1,),
            in_specs=[
                pl.BlockSpec(arrived.shape, lambda i, c: (0, 0, 0)),
                pl.BlockSpec((feats, half), lambda i, c: (0, c[0])),
                pl.BlockSpec((feats, half), lambda i, c: (0, 1 - c[0])),
                pl.BlockSpec(rank_of.shape, fixed),
            ],
            out_specs=[pl.BlockSpec((slots_all, half), fixed)] * 2,
            scratch_shapes=[pltpu.VMEM((4 * kinds.shape[1], kinds.shape[2]), bf16)],
        ),
        compiler_params=BIG,
    )(
        jnp.stack([core, group]).astype(jnp.int32),
        arrived,
        down,
        down,
        rank_of,
    )
    on_chip = whole(sum_kernel, product, kept, swap(sent, "c"))
    pieces = over_x(on_chip.reshape(chips, slots_all // chips, half))
    near = over_x(
        whole(add_kernel, jax.ShapeDtypeStruct(pieces.shape, bf16), pieces)
    ).reshape(slots_all, half)
    far = swap(near, "c")

    def routes_of(side, near, far):
        rows_of = lambda i, c: (side, 0)
        hidden_of = lambda i, c: (side, c[0] ^ i)
        weights_of = lambda i, c: (0, c[0] ^ i)
        return pl.pallas_call(
            functools.partial(route_kernel, capacity),
            out_shape=block,
            grid_spec=pltpu.PrefetchScalarGridSpec(
                num_scalar_prefetch=1,
                grid=(2,),
                in_specs=[
                    pl.BlockSpec((slots_side, half), rows_of),
                    pl.BlockSpec((slots_side, half), rows_of),
                    pl.BlockSpec((slots_side, half), hidden_of),
                    pl.BlockSpec((slots_side, half), hidden_of),
                    pl.BlockSpec((feats, half), weights_of),
                    pl.BlockSpec((feats, half), weights_of),
                    pl.BlockSpec(put_all.shape, fixed),
                    pl.BlockSpec(rank_of.shape, fixed),
                ],
                out_specs=block_spec,
                scratch_shapes=[
                    pltpu.VMEM((slots_side, feats), jnp.float32),
                    pltpu.VMEM((slots_side, 1), jnp.float32),
                ],
            ),
            compiler_params=BIG,
        )(cores, near, far, gate_rows, up_rows, w_gate[0], w_up[0], put_all, rank_of)

    pair_routes = routes_of(1, near, far)
    pair_back = swap(pair_routes, "yl")
    far, _ = lax.optimization_barrier((far, pair_routes))
    own_routes = routes_of(0, near, far)
    both = whole(sum_kernel, block, own_routes, pair_back)
    returned = over_group(both)
    grad_in, grad_prob = whole(
        functools.partial(combine_kernel, capacity),
        (
            jax.ShapeDtypeStruct((feats, tokens), bf16),
            jax.ShapeDtypeStruct((2, tokens), bf16),
        ),
        returned,
        routes,
        gate_prob.T,
        widen,
        expert_of,
        rank_of,
        pick_all,
    )
    return (grad_in.T, grad_prob.T)


def solution(mesh):
    nodes, local = mesh.devices.shape
    rows = 8
    fine = Mesh(mesh.devices.reshape(nodes // rows, rows // 2, 2, local // 2, 2), (*NODE, "x", "c"))
    node, feats = NODE, ("x", "c")
    return jax.shard_map(
        shards,
        mesh=fine,
        in_specs=(
            P(node, feats),
            P(node, None),
            P(node, None),
            P(node, None, None),
            P(node, None, None),
            P(node, feats, None),
            P(node, feats, None),
            P(node, None, feats),
        ),
        out_specs=(P(node, feats), P(node, None)),
        check_vma=False,
    )
```
